256 devices in a mesh: gx: 32 (over z, y_hi, core), gz: 8 (over y_lo, x).
Axes of the slice: x: 4, y: 4 (y_hi: 2, y_lo: 2; y = y_hi * 2 + y_lo), z: 8, core: 2. Of those that a mesh axis runs over, the one named last changes fastest.
Arguments:
- density: float32 [4096, 8, 1024], P('gx', None, 'gz'), may hold values from 0.5 to 2
- momentum: float32 [3, 4096, 8, 1024], P(None, 'gx', None, 'gz'), may hold values from -3 to 3
- energy: float32 [4096, 8, 1024], P('gx', None, 'gz'), may hold values from 2 to 4
- costate: float32 [5, 4096, 8, 1024], P(None, 'gx', None, 'gz'), may hold values from -6 to 6
Outputs:
- adjoint: float32 [5, 4096, 8, 1024], P(None, 'gx', None, 'gz')
The draws below stay inside these ranges and needn't reach their ends.
All inputs are finite; a program needn't handle non-finite values.
Results may differ from the reference program's by a relative error of at most 0.00005.
Values sent between devices are 32-bit elements; how exact they have to be, the bound alone decides.
No kernel may reach another device: no remote copies, remote signals or barrier semaphores. Data moves between devices by JAX's collectives and lax.ppermute only.
A program may use at most 128 MiB of HBM per device.

```python
import math
import jax
import jax.numpy as jnp
from jax import lax

NX = 4096
NZ = 1024
NY = 8


def block_levels(rng, shape, pieces, low, top_value):
    def one(axis_at, blocks):
        heights = jax.random.uniform(jax.random.fold_in(jax.random.fold_in(rng, 6), axis_at), (blocks,), jnp.float32, low / len(pieces), top_value / len(pieces))
        return jnp.repeat(jnp.exp(heights), shape[axis_at] // blocks).reshape((-1,) + (1,) * (len(shape) - axis_at - 1))

    gain = one(*pieces[0])
    for cut in pieces[1:]:
        gain = gain * one(*cut)
    return gain


def normal_values(stream_key, dims, width, limit, pieces=(), kind=jnp.bfloat16):
    values = width * jax.random.normal(stream_key, dims, jnp.float32)
    if pieces:
        values = values * block_levels(stream_key, dims, pieces, -0.22, 0.18)
    return jnp.clip(values, -limit, limit).astype(kind)


def setup_inputs(seed: int = 0) -> dict:
    keys = jax.random.split(jax.random.key(seed), 5)
    density = jnp.clip(0.5 + 1.5 * jax.random.uniform(keys[0], (NX, NY, NZ), jnp.float32) ** block_levels(keys[0], (NX, NY, NZ), ((0, 32), (2, 8)), -0.2, 0.2), 0.5, 2.0)
    momentum = normal_values(keys[1], (3, NX, NY, NZ), 0.5, 3.0, ((1, 32), (3, 8)), jnp.float32)
    energy = jnp.clip(2.0 + 2.0 * jax.random.uniform(keys[2], (NX, NY, NZ), jnp.float32) ** block_levels(keys[2], (NX, NY, NZ), ((0, 32), (2, 8)), -0.2, 0.2), 2.0, 4.0)
    costate = normal_values(keys[3], (5, NX, NY, NZ), 1.0, 6.0, ((1, 32), (3, 8)), jnp.float32)
    return {"density": density, "momentum": momentum, "energy": energy, "costate": costate}


pade_alpha = 1.0 / 3.0
near_coef = 14.0 / 9.0
far_coef = 1.0 / 9.0
step_scale = 0.1
gas_gamma = 1.4

def fluxes(density, momentum, energy):
    inverse = 1.0 / density
    speed_stream = momentum[0] * inverse
    speed_span = momentum[2] * inverse
    kinetic = 0.5 * (momentum[0] * momentum[0] + momentum[1] * momentum[1] + momentum[2] * momentum[2]) * inverse
    pressure = (gas_gamma - 1.0) * (energy - kinetic)
    enthalpy = energy + pressure
    flux_stream = jnp.stack([momentum[0], momentum[0] * speed_stream + pressure, momentum[1] * speed_stream, momentum[2] * speed_stream, enthalpy * speed_stream])
    flux_span = jnp.stack([momentum[2], momentum[0] * speed_span, momentum[1] * speed_span, momentum[2] * speed_span + pressure, enthalpy * speed_span])
    return (flux_stream, flux_span)

def compact(values, line_axis):
    length = values.shape[line_axis]
    angles = 2.0 * math.pi * jnp.arange(length // 2 + 1) / length
    symbol = (near_coef * jnp.sin(angles) + 0.5 * far_coef * jnp.sin(2.0 * angles)) / (1.0 + 2.0 * pade_alpha * jnp.cos(angles))
    layout = [1, 1, 1]
    layout[line_axis] = length // 2 + 1
    spectrum = jnp.fft.rfft(values, axis=line_axis)
    return jnp.fft.irfft(spectrum * (1j * symbol).reshape(layout), n=length, axis=line_axis).astype(values.dtype)

def pullback(density, momentum, energy, slope_stream, slope_span):
    primal_out, pullback_fn = jax.vjp(fluxes, density, momentum, energy)
    gradients = pullback_fn((slope_stream, slope_span))
    return jnp.concatenate([gradients[0][None], gradients[1], gradients[2][None]], 0)

def reference(density, momentum, energy, costate):
    slope_stream = lax.map(lambda component: compact(component, 0), costate)
    slope_span = lax.map(lambda component: compact(component, 2), costate)

    def per_plane(plane_at):
        slab_of = lambda values: lax.dynamic_slice_in_dim(values, plane_at, 1, values.ndim - 2)
        result = pullback(slab_of(density), slab_of(momentum), slab_of(energy), slab_of(slope_stream), slab_of(slope_span))
        return result[:, :, 0, :]
    stacked = lax.map(per_plane, jnp.arange(NY, dtype=jnp.int32))
    pulled = jnp.transpose(stacked, (1, 2, 0, 3))
    return costate + step_scale * pulled
```

```python
import math

import jax
import jax.numpy as jnp
import ml_dtypes
import numpy as np
from jax import lax
from jax.experimental import pallas as pl
from jax.experimental.pallas import tpu as pltpu
from jax.sharding import PartitionSpec as P

pade_alpha = 1.0 / 3.0
near_coef = 14.0 / 9.0
far_coef = 1.0 / 9.0
step_scale = 0.1
gas_gamma = 1.4

root = (-1.0 + math.sqrt(1.0 - 4.0 * pade_alpha * pade_alpha)) / (2.0 * pade_alpha)
side = 0.25 * far_coef / pade_alpha
tail = (0.5 * near_coef - side) / pade_alpha

fields = 5
segments = 8
vmem_bytes = 48 * 1024 * 1024


def split(values):
    high = values.astype(ml_dtypes.bfloat16)
    low = (values - high.astype(np.float64)).astype(ml_dtypes.bfloat16)
    return high, low


def end_weights(length):
    cell = np.arange(length, dtype=np.float64)
    rows = np.zeros((4, length))
    rows[0] = root ** (length - cell)
    rows[1, length - 1] = 1.0
    rows[2] = root ** (cell + 1.0)
    rows[3, 0] = 1.0
    return rows


def stack_ends(rows):
    high, low = split(rows)
    stacked = np.zeros((16, rows.shape[1]), ml_dtypes.bfloat16)
    stacked[0:4] = high
    stacked[8:12] = low
    return stacked


def local_matrix(length):
    cell = np.arange(length)
    gap = cell[None, :] - cell[:, None]
    reach = np.abs(gap).astype(np.float64)
    taps = np.where(reach > 0, tail * root**reach, 0.0) - np.where(reach == 1, side, 0.0)
    high, low = split(np.sign(gap) * taps)
    return np.concatenate(
        [np.concatenate([high, low], 1), np.concatenate([high, low], 1)], 0
    )


def arrival_rows(length):
    cell = np.arange(length, dtype=np.float64)
    rows = np.zeros((4, length))
    rows[0] = tail * root**cell
    rows[1, 0] = -side
    rows[2] = -tail * root ** (length - 1.0 - cell)
    rows[3, length - 1] = side
    return rows


def stack_arrival(rows):
    high, low = split(rows)
    return np.concatenate([high, high, low, np.zeros_like(high)], 0)


def ends_kernel(rows, costate_hbm, weights_ref, even_x_ref, odd_x_ref, even_z_ref, odd_z_ref, held, sems):
    per_segment = rows // segments
    copies = [
        pltpu.make_async_copy(costate_hbm.at[c], held.at[c], sems.at[c]) for c in range(fields)
    ]
    for copy in copies:
        copy.start()
    x_even = lax.axis_index("gx") % 2 == 0
    z_even = lax.axis_index("gz") % 2 == 0
    weights = weights_ref[...]
    for c in range(fields):
        copies[c].wait()
        ahead = held[c, :, 0]
        back = held[c, :, per_segment - 1]
        for j in range(1, per_segment):
            ahead = ahead * root + held[c, :, j]
            back = back * root + held[c, :, per_segment - 1 - j]
        to_right = ahead[segments - 1] * root
        to_left = back[0] * root
        for s in range(1, segments):
            to_right = to_right + ahead[segments - 1 - s] * float(root ** (1 + s * per_segment))
            to_left = to_left + back[s] * float(root ** (1 + s * per_segment))
        first = held[c, 0, 0]
        last = held[c, segments - 1, per_segment - 1]
        even_x_ref[c, 0] = jnp.where(x_even, to_right, to_left)
        even_x_ref[c, 1] = jnp.where(x_even, last, first)
        odd_x_ref[c, 0] = jnp.where(x_even, to_left, to_right)
        odd_x_ref[c, 1] = jnp.where(x_even, first, last)
        lines = held[c].reshape(-1, 128)
        high = lines.astype(jnp.bfloat16)
        low = (lines - high.astype(jnp.float32)).astype(jnp.bfloat16)
        dims = (((1,), (1,)), ((), ()))
        sums = lax.dot_general(weights, high, dims, preferred_element_type=jnp.float32)
        sums = sums + lax.dot_general(weights, low, dims, preferred_element_type=jnp.float32)
        sums = sums[0:8] + sums[8:16]
        even_z_ref[c] = jnp.where(z_even, sums[0:2], sums[2:4])
        odd_z_ref[c] = jnp.where(z_even, sums[2:4], sums[0:2])


def pull(a, b, u0, u1, u2, h, k):
    a4u0 = a[4] * u0
    b4u2 = b[4] * u2
    both = a4u0 + b4u2
    g = (gas_gamma - 1.0) * (a[1] + b[3] + both)
    a1u0 = a[1] * u0
    b3u2 = b[3] * u2
    v0 = a1u0 + a[2] * u1 + a[3] * u2 + a[4] * h
    v2 = b[1] * u0 + b[2] * u1 + b3u2 + b[4] * h
    mass = g * k - v0 * u0 - v2 * u2
    m0 = a[0] + a1u0 + b[1] * u2 + v0 - g * u0
    m1 = a[2] * u0 + b[2] * u2 - g * u1
    m2 = b[0] + a[3] * u0 + b3u2 + v2 - g * u2
    energy = both + g
    return [mass, m0, m1, m2, energy]


def local_kernel(
    rows, density_ref, momentum_ref, energy_ref, costate_ref, matrix_ref, partial_ref, coef_ref, behind, span
):
    matrix = matrix_ref[...]
    for c in range(fields):
        lines = costate_ref[c].reshape(-1, 128)
        high = lines.astype(jnp.bfloat16)
        low = (lines - high.astype(jnp.float32)).astype(jnp.bfloat16)
        out = jnp.dot(
            jnp.concatenate([high, low], 1), matrix, preferred_element_type=jnp.float32
        )
        span[c] = (out[:, :128] + out[:, 128:]).reshape(rows, 8, 128)

    def backward(step, carry):
        i = rows - 1 - step
        nxt = []
        for c in range(fields):
            behind[c, i] = carry[c]
            nxt.append(carry[c] * root + costate_ref[c, i] * (tail * root))
        return tuple(nxt)

    zero = jnp.zeros((8, 128), jnp.float32)
    lax.fori_loop(0, rows, backward, (zero,) * fields, unroll=8)

    def forward(i, carry):
        ahead, before, now = carry
        upper = jnp.minimum(i + 1, rows - 1)
        more = jnp.where(i + 1 < rows, 1.0, 0.0).astype(jnp.float32)
        inverse = 1.0 / density_ref[i]
        u0 = momentum_ref[0, i] * inverse
        u1 = momentum_ref[1, i] * inverse
        u2 = momentum_ref[2, i] * inverse
        k = 0.5 * (u0 * u0 + u1 * u1 + u2 * u2)
        h = gas_gamma * (energy_ref[i] * inverse) - (gas_gamma - 1.0) * k
        after = [costate_ref[c, upper] * more for c in range(fields)]
        a = [
            (ahead[c] - behind[c, i]) + side * (after[c] - before[c]) for c in range(fields)
        ]
        b = [span[c, i] for c in range(fields)]
        pulled = pull(a, b, u0, u1, u2, h, k)
        for c in range(fields):
            partial_ref[c, i] = now[c] + step_scale * pulled[c]
        for slot, value in enumerate((u0, u1, u2, h, k)):
            coef_ref[slot, i] = value
        ahead = tuple(ahead[c] * root + now[c] * (tail * root) for c in range(fields))
        return ahead, now, tuple(after)

    start = tuple(costate_ref[c, 0] for c in range(fields))
    lax.fori_loop(0, rows, forward, ((zero,) * fields, (zero,) * fields, start), unroll=4)


def join_kernel(
    rows, partial_ref, coef_ref, even_x_ref, odd_x_ref, even_z_ref, odd_z_ref, arrive_ref, scale_ref, out_ref, span
):
    x_even = lax.axis_index("gx") % 2 == 0
    z_even = lax.axis_index("gz") % 2 == 0
    arrive = arrive_ref[...]
    for c in range(fields):
        even = even_z_ref[c]
        odd = odd_z_ref[c]
        values = jnp.concatenate(
            [jnp.where(z_even, odd, even), jnp.where(z_even, even, odd)], 0
        )
        high = values.astype(jnp.bfloat16).astype(jnp.float32)
        low = values - high
        stacked = jnp.concatenate([high, low, high, jnp.zeros_like(high)], 0)
        columns = jnp.swapaxes(stacked, 0, 1).astype(jnp.bfloat16)
        span[c] = jnp.dot(columns, arrive, preferred_element_type=jnp.float32).reshape(rows, 8, 128)
    left_sum = [jnp.where(x_even, odd_x_ref[c, 0], even_x_ref[c, 0]) for c in range(fields)]
    right_sum = [jnp.where(x_even, even_x_ref[c, 0], odd_x_ref[c, 0]) for c in range(fields)]

    def add(i, a):
        u0, u1, u2, h, k = [coef_ref[slot, i] for slot in range(5)]
        b = [span[c, i] for c in range(fields)]
        pulled = pull(a, b, u0, u1, u2, h, k)
        for c in range(fields):
            out_ref[c, i] = partial_ref[c, i] + step_scale * pulled[c]

    def stream(i):
        return [left_sum[c] * scale_ref[0, i] + right_sum[c] * scale_ref[1, i] for c in range(fields)]

    def body(i, carry):
        add(i, stream(i))
        return carry

    first = stream(0)
    last = stream(rows - 1)
    for c in range(fields):
        left_edge = jnp.where(x_even, odd_x_ref[c, 1], even_x_ref[c, 1])
        right_edge = jnp.where(x_even, even_x_ref[c, 1], odd_x_ref[c, 1])
        first[c] = first[c] - side * left_edge
        last[c] = last[c] + side * right_edge
    add(0, first)
    lax.fori_loop(1, rows - 1, body, 0, unroll=3)
    add(rows - 1, last)


def per_device(density, momentum, energy, costate):
    rows, planes, cells = density.shape
    f32 = jnp.float32
    whole = pl.BlockSpec(memory_space=pltpu.VMEM)
    params = pltpu.CompilerParams(vmem_limit_bytes=vmem_bytes)
    x_shape = jax.ShapeDtypeStruct((fields, 2, planes, cells), f32)
    z_shape = jax.ShapeDtypeStruct((fields, 2, rows * planes), f32)
    block = jax.ShapeDtypeStruct((fields, rows, planes, cells), f32)
    per_segment = rows // segments

    even_x, odd_x, even_z, odd_z = pl.pallas_call(
        lambda *refs: ends_kernel(rows, *refs),
        out_shape=(x_shape, x_shape, z_shape, z_shape),
        in_specs=[pl.BlockSpec(memory_space=pl.ANY), whole],
        out_specs=(whole,) * 4,
        scratch_shapes=[
            pltpu.VMEM((fields, segments, per_segment, planes, cells), f32),
            pltpu.SemaphoreType.DMA((fields,)),
        ],
        compiler_params=params,
        name="ends",
    )(
        costate.reshape(fields, segments, per_segment, planes, cells),
        jnp.asarray(stack_ends(end_weights(cells))),
    )

    def pairs(values, axis, odd):
        count = lax.axis_size(axis)
        links = []
        for i in range(odd, count + odd, 2):
            a, b = i % count, (i + 1) % count
            links += [(a, b), (b, a)]
        return lax.ppermute(values, axis, links)

    even_x = pairs(even_x, "gx", 0)
    even_z = pairs(even_z, "gz", 0)
    odd_z = pairs(odd_z, "gz", 1)
    odd_x = pairs(odd_x, "gx", 1)

    partial, coef = pl.pallas_call(
        lambda *refs: local_kernel(rows, *refs),
        out_shape=(block, block),
        in_specs=[whole] * 5,
        out_specs=(whole,) * 2,
        scratch_shapes=[
            pltpu.VMEM((fields, rows, planes, cells), f32),
            pltpu.VMEM((fields, rows, planes, cells), f32),
        ],
        compiler_params=params,
        cost_estimate=pl.CostEstimate(flops=300_000_000, bytes_accessed=10_000_000, transcendentals=0),
        name="local",
    )(density, momentum, energy, costate, jnp.asarray(local_matrix(cells)))

    rows_x = arrival_rows(rows)
    scale = jnp.asarray(rows_x[0::2].astype(np.float32))
    return pl.pallas_call(
        lambda *refs: join_kernel(rows, *refs),
        out_shape=block,
        in_specs=[whole] * 7 + [pl.BlockSpec(memory_space=pltpu.SMEM)],
        out_specs=whole,
        scratch_shapes=[pltpu.VMEM((fields, rows, planes, cells), f32)],
        compiler_params=params,
        name="join",
    )(
        partial,
        coef,
        even_x,
        odd_x,
        even_z,
        odd_z,
        jnp.asarray(stack_arrival(arrival_rows(cells))),
        scale,
    )


def solution(mesh):
    return jax.shard_map(
        per_device,
        mesh=mesh,
        in_specs=(
            P("gx", None, "gz"),
            P(None, "gx", None, "gz"),
            P("gx", None, "gz"),
            P(None, "gx", None, "gz"),
        ),
        out_specs=P(None, "gx", None, "gz"),
        check_vma=False,
    )
```

```python
import math

import jax
import jax.numpy as jnp
import ml_dtypes
import numpy as np
from jax import lax
from jax.experimental import pallas as pl
from jax.experimental.pallas import tpu as pltpu
from jax.sharding import PartitionSpec as P

pade_alpha = 1.0 / 3.0
near_coef = 14.0 / 9.0
far_coef = 1.0 / 9.0
step_scale = 0.1
gas_gamma = 1.4

root = (-1.0 + math.sqrt(1.0 - 4.0 * pade_alpha * pade_alpha)) / (2.0 * pade_alpha)
side = 0.25 * far_coef / pade_alpha
tail = (0.5 * near_coef - side) / pade_alpha

fields = 5
segments = 8
vmem_bytes = 16 * 1024 * 1024


def split(values):
    high = values.astype(ml_dtypes.bfloat16)
    low = (values - high.astype(np.float64)).astype(ml_dtypes.bfloat16)
    return high, low


def end_weights(length):
    cell = np.arange(length, dtype=np.float64)
    rows = np.zeros((4, length))
    rows[0] = root ** (length - cell)
    rows[1, length - 1] = 1.0
    rows[2] = root ** (cell + 1.0)
    rows[3, 0] = 1.0
    return rows


def stack_ends(rows):
    high, low = split(rows)
    stacked = np.zeros((16, rows.shape[1]), ml_dtypes.bfloat16)
    stacked[0:4] = high
    stacked[8:12] = low
    return stacked


def local_matrix(length):
    cell = np.arange(length)
    gap = cell[None, :] - cell[:, None]
    reach = np.abs(gap).astype(np.float64)
    taps = np.where(reach > 0, tail * root**reach, 0.0) - np.where(reach == 1, side, 0.0)
    high, low = split(step_scale * np.sign(gap) * taps)
    return np.concatenate(
        [np.concatenate([high, low], 1), np.concatenate([high, low], 1)], 0
    )


def arrival_rows(length):
    cell = np.arange(length, dtype=np.float64)
    rows = np.zeros((4, length))
    rows[0] = tail * root**cell
    rows[1, 0] = -side
    rows[2] = -tail * root ** (length - 1.0 - cell)
    rows[3, length - 1] = side
    return rows


def stack_arrival(rows):
    high, low = split(rows)
    return np.concatenate([high, high, low, np.zeros_like(high)], 0)


def in_hbm(values):
    return pltpu.with_memory_space_constraint(values, pltpu.HBM)


def ends_kernel(
    rows, costate_hbm, weights_hbm, held, even_x_ref, even_z_ref, odd_z_ref, odd_x_ref, weights_ref, sems
):
    per_segment = rows // segments
    weights_copy = pltpu.make_async_copy(weights_hbm, weights_ref, sems.at[fields])
    copies = [
        pltpu.make_async_copy(costate_hbm.at[c], held.at[c], sems.at[c]) for c in range(fields)
    ]
    weights_copy.start()
    for copy in copies:
        copy.start()
    x_even = lax.axis_index("gx") % 2 == 0
    z_even = lax.axis_index("gz") % 2 == 0
    weights_copy.wait()

    def component(c, carry):
        pltpu.make_async_copy(costate_hbm.at[c], held.at[c], sems.at[c]).wait()
        weights = weights_ref[...]
        ahead = held[c, :, 0]
        back = held[c, :, per_segment - 1]
        for j in range(1, per_segment):
            ahead = ahead * root + held[c, :, j]
            back = back * root + held[c, :, per_segment - 1 - j]
        to_right = ahead[segments - 1] * root
        to_left = back[0] * root
        for s in range(1, segments):
            to_right = to_right + ahead[segments - 1 - s] * float(root ** (1 + s * per_segment))
            to_left = to_left + back[s] * float(root ** (1 + s * per_segment))
        first = held[c, 0, 0]
        last = held[c, segments - 1, per_segment - 1]
        even_x_ref[c, 0] = jnp.where(x_even, to_right, to_left)
        even_x_ref[c, 1] = jnp.where(x_even, last, first)
        odd_x_ref[c, 0] = jnp.where(x_even, to_left, to_right)
        odd_x_ref[c, 1] = jnp.where(x_even, first, last)
        lines = held[c].reshape(-1, 128)
        high = lines.astype(jnp.bfloat16)
        low = (lines - high.astype(jnp.float32)).astype(jnp.bfloat16)
        dims = (((1,), (1,)), ((), ()))
        sums = lax.dot_general(weights, high, dims, preferred_element_type=jnp.float32)
        sums = sums + lax.dot_general(weights, low, dims, preferred_element_type=jnp.float32)
        sums = sums[0:8] + sums[8:16]
        even_z_ref[c] = jnp.where(z_even, sums[0:2], sums[2:4])
        odd_z_ref[c] = jnp.where(z_even, sums[2:4], sums[0:2])
        return carry

    lax.fori_loop(0, fields, component, 0)


def pull(a, b, u0, u1, u2, h, k):
    a4u0 = a[4] * u0
    b4u2 = b[4] * u2
    both = a4u0 + b4u2
    g = (gas_gamma - 1.0) * (a[1] + b[3] + both)
    a1u0 = a[1] * u0
    b3u2 = b[3] * u2
    v0 = a1u0 + a[2] * u1 + a[3] * u2 + a[4] * h
    v2 = b[1] * u0 + b[2] * u1 + b3u2 + b[4] * h
    mass = g * k - v0 * u0 - v2 * u2
    m0 = a[0] + a1u0 + b[1] * u2 + v0 - g * u0
    m1 = a[2] * u0 + b[2] * u2 - g * u1
    m2 = b[0] + a[3] * u0 + b3u2 + v2 - g * u2
    energy = both + g
    return [mass, m0, m1, m2, energy]


def local_kernel(
    rows, costate_ref, matrix_hbm, density_hbm, momentum_hbm, energy_hbm, partial_ref, coef_ref,
    behind, span, matrix_ref, density_ref, momentum_ref, energy_ref, sems,
):
    copies = [
        pltpu.make_async_copy(source, target, sems.at[n])
        for n, (source, target) in enumerate(
            (
                (matrix_hbm, matrix_ref),
                (density_hbm, density_ref),
                (momentum_hbm, momentum_ref),
                (energy_hbm, energy_ref),
            )
        )
    ]
    for copy in copies:
        copy.start()
    zero = jnp.zeros((8, 128), jnp.float32)
    gain = step_scale * tail
    edge = step_scale * side
    for c in range(fields):
        behind[c, rows - 1] = zero
    zero = behind[0, rows - 1]

    def backward(step, carry):
        i = rows - 2 - step
        nxt = []
        for c in range(fields):
            after = costate_ref[c, i + 1]
            now = carry[c] * root + after * (gain * root)
            behind[c, i] = now - after * edge
            nxt.append(now)
        return tuple(nxt)

    lax.fori_loop(0, rows - 1, backward, (zero,) * fields, unroll=8)
    copies[0].wait()

    def across(c, carry):
        lines = costate_ref[c].reshape(-1, 128)
        high = lines.astype(jnp.bfloat16)
        low = (lines - high.astype(jnp.float32)).astype(jnp.bfloat16)
        out = jnp.dot(
            jnp.concatenate([high, low], 1), matrix_ref[...], preferred_element_type=jnp.float32
        )
        span[c] = (out[:, :128] + out[:, 128:]).reshape(rows, 8, 128)
        return carry

    lax.fori_loop(0, fields, across, 0)
    for copy in copies[1:]:
        copy.wait()

    def forward(i, carry):
        ahead, before = carry
        rho = density_ref[i]
        inverse = pl.reciprocal(rho, approx=True)
        inverse = inverse * (2.0 - rho * inverse)
        inverse = inverse * (2.0 - rho * inverse)
        u0 = momentum_ref[0, i] * inverse
        u1 = momentum_ref[1, i] * inverse
        u2 = momentum_ref[2, i] * inverse
        k = 0.5 * (u0 * u0 + u1 * u1 + u2 * u2)
        h = gas_gamma * (energy_ref[i] * inverse) - (gas_gamma - 1.0) * k
        ahead = tuple(ahead[c] * root + before[c] * (gain * root) for c in range(fields))
        a = [ahead[c] - before[c] * edge - behind[c, i] for c in range(fields)]
        b = [span[c, i] for c in range(fields)]
        pulled = pull(a, b, u0, u1, u2, h, k)
        now = tuple(costate_ref[c, i] for c in range(fields))
        for c in range(fields):
            partial_ref[c, i] = now[c] + pulled[c]
        for slot, value in enumerate((u0, u1, u2, h, k)):
            coef_ref[slot, i] = value
        return ahead, now

    lax.fori_loop(0, rows, forward, ((zero,) * fields, (zero,) * fields), unroll=4)


def join_kernel(
    rows, partial_ref, coef_ref, even_x_ref, even_z_ref, odd_z_ref, odd_x_ref, arrive_ref, scale_ref,
    out_hbm, result, sems,
):
    x_even = lax.axis_index("gx") % 2 == 0
    z_even = lax.axis_index("gz") % 2 == 0
    per_segment = rows // segments
    wide = per_segment * 8
    left_sum = [jnp.where(x_even, odd_x_ref[c, 0], even_x_ref[c, 0]) for c in range(fields)]
    right_sum = [jnp.where(x_even, even_x_ref[c, 0], odd_x_ref[c, 0]) for c in range(fields)]

    def copy_out(s):
        part = pl.ds(s * per_segment, per_segment)
        return pltpu.make_async_copy(result.at[:, part], out_hbm.at[:, part], sems.at[s])

    def segment(s, carry):
        arrive = arrive_ref[...]
        lanes = pl.ds(pl.multiple_of(s * wide, wide), wide)
        span = []
        for c in range(fields):
            even = even_z_ref[c, :, lanes]
            odd = odd_z_ref[c, :, lanes]
            values = jnp.concatenate(
                [jnp.where(z_even, odd, even), jnp.where(z_even, even, odd)], 0
            )
            high = values.astype(jnp.bfloat16).astype(jnp.float32)
            low = values - high
            stacked = jnp.concatenate([high, low, high, jnp.zeros_like(high)], 0)
            columns = jnp.swapaxes(stacked, 0, 1).astype(jnp.bfloat16)
            span.append(
                jnp.dot(columns, arrive, preferred_element_type=jnp.float32).reshape(per_segment, 8, 128)
            )
        for j in range(per_segment):
            i = s * per_segment + j
            a = [left_sum[c] * scale_ref[0, i] + right_sum[c] * scale_ref[1, i] for c in range(fields)]
            if j == 0:
                edge = jnp.where(s == 0, -step_scale * side, 0.0).astype(jnp.float32)
                for c in range(fields):
                    a[c] = a[c] + edge * jnp.where(x_even, odd_x_ref[c, 1], even_x_ref[c, 1])
            if j == per_segment - 1:
                edge = jnp.where(s == segments - 1, step_scale * side, 0.0).astype(jnp.float32)
                for c in range(fields):
                    a[c] = a[c] + edge * jnp.where(x_even, even_x_ref[c, 1], odd_x_ref[c, 1])
            b = [span[c][j] for c in range(fields)]
            pulled = pull(a, b, *[coef_ref[slot, i] for slot in range(5)])
            for c in range(fields):
                result[c, i] = partial_ref[c, i] + pulled[c]
        copy_out(s).start()
        return carry

    lax.fori_loop(0, segments, segment, 0)

    def finish(s, carry):
        copy_out(s).wait()
        return carry

    lax.fori_loop(0, segments, finish, 0)


def per_device(density, momentum, energy, costate):
    rows, planes, cells = density.shape
    f32 = jnp.float32
    whole = pl.BlockSpec(memory_space=pltpu.VMEM)
    hbm = pl.BlockSpec(memory_space=pltpu.HBM)
    params = pltpu.CompilerParams(vmem_limit_bytes=vmem_bytes)
    x_shape = jax.ShapeDtypeStruct((fields, 2, planes, cells), f32)
    z_shape = jax.ShapeDtypeStruct((fields, 2, rows * planes), f32)
    block = jax.ShapeDtypeStruct((fields, rows, planes, cells), f32)
    per_segment = rows // segments

    held, even_x, even_z, odd_z, odd_x = pl.pallas_call(
        lambda *refs: ends_kernel(rows, *refs),
        out_shape=(
            jax.ShapeDtypeStruct((fields, segments, per_segment, planes, cells), f32),
            x_shape,
            z_shape,
            z_shape,
            x_shape,
        ),
        in_specs=[hbm, hbm],
        out_specs=(whole,) * 5,
        scratch_shapes=[
            pltpu.VMEM((16, cells), jnp.bfloat16),
            pltpu.SemaphoreType.DMA((fields + 1,)),
        ],
        compiler_params=params,
        name="ends",
    )(
        in_hbm(costate.reshape(fields, segments, per_segment, planes, cells)),
        in_hbm(jnp.asarray(stack_ends(end_weights(cells)))),
    )

    def pairs(values, axis, odd):
        count = lax.axis_size(axis)
        links = []
        for i in range(odd, count + odd, 2):
            a, b = i % count, (i + 1) % count
            links += [(a, b), (b, a)]
        return lax.ppermute(values, axis, links)

    even_x = pairs(even_x, "gx", 0)
    even_z = pairs(even_z, "gz", 0)
    odd_z = pairs(odd_z, "gz", 1)
    odd_x = pairs(odd_x, "gx", 1)

    matrix = local_matrix(cells)
    partial, coef = pl.pallas_call(
        lambda *refs: local_kernel(rows, *refs),
        out_shape=(block, block),
        in_specs=[whole] + [hbm] * 4,
        out_specs=(whole,) * 2,
        scratch_shapes=[
            pltpu.VMEM((fields, rows, planes, cells), f32),
            pltpu.VMEM((fields, rows, planes, cells), f32),
            pltpu.VMEM(matrix.shape, jnp.bfloat16),
            pltpu.VMEM((rows, planes, cells), f32),
            pltpu.VMEM((3, rows, planes, cells), f32),
            pltpu.VMEM((rows, planes, cells), f32),
            pltpu.SemaphoreType.DMA((4,)),
        ],
        compiler_params=params,
        cost_estimate=pl.CostEstimate(flops=300_000_000, bytes_accessed=10_000_000, transcendentals=0),
        name="local",
    )(
        held.reshape(costate.shape),
        in_hbm(jnp.asarray(matrix)),
        in_hbm(density),
        in_hbm(momentum),
        in_hbm(energy),
    )

    scale = jnp.asarray((step_scale * arrival_rows(rows)[0::2]).astype(np.float32))
    return pl.pallas_call(
        lambda *refs: join_kernel(rows, *refs),
        out_shape=block,
        in_specs=[whole] * 7 + [pl.BlockSpec(memory_space=pltpu.SMEM)],
        out_specs=hbm,
        scratch_shapes=[
            pltpu.VMEM((fields, rows, planes, cells), f32),
            pltpu.SemaphoreType.DMA((segments,)),
        ],
        compiler_params=params,
        name="join",
    )(
        partial,
        coef,
        even_x,
        even_z,
        odd_z,
        odd_x,
        jnp.asarray(stack_arrival(step_scale * arrival_rows(cells))),
        scale,
    )


def solution(mesh):
    return jax.shard_map(
        per_device,
        mesh=mesh,
        in_specs=(
            P("gx", None, "gz"),
            P(None, "gx", None, "gz"),
            P("gx", None, "gz"),
            P(None, "gx", None, "gz"),
        ),
        out_specs=P(None, "gx", None, "gz"),
        check_vma=False,
    )
```

```python
import math

import jax
import jax.numpy as jnp
import ml_dtypes
import numpy as np
from jax import lax
from jax.experimental import pallas as pl
from jax.experimental.pallas import tpu as pltpu
from jax.sharding import PartitionSpec as P

pade_alpha = 1.0 / 3.0
near_coef = 14.0 / 9.0
far_coef = 1.0 / 9.0
step_scale = 0.1
gas_gamma = 1.4

root = (-1.0 + math.sqrt(1.0 - 4.0 * pade_alpha * pade_alpha)) / (2.0 * pade_alpha)
side = 0.25 * far_coef / pade_alpha
tail = (0.5 * near_coef - side) / pade_alpha

fields = 5
segments = 8
arrival_depth = 24
vmem_bytes = 16 * 1024 * 1024


def split(values):
    high = values.astype(ml_dtypes.bfloat16)
    low = (values - high.astype(np.float64)).astype(ml_dtypes.bfloat16)
    return high, low


def end_weights(length):
    cell = np.arange(length, dtype=np.float64)
    rows = np.zeros((4, length))
    rows[0] = root ** (length - cell)
    rows[1, length - 1] = 1.0
    rows[2] = root ** (cell + 1.0)
    rows[3, 0] = 1.0
    return rows


def stack_ends(rows):
    stacked = np.zeros((2, 16, 2 * rows.shape[1]), ml_dtypes.bfloat16)
    for place, order in enumerate(((0, 1, 2, 3), (2, 3, 0, 1))):
        high, low = split(rows[list(order)])
        stacked[place, 0:4] = np.concatenate([high, high], 1)
        stacked[place, 8:12] = np.concatenate([low, np.zeros_like(low)], 1)
    return stacked


def local_matrix(length):
    cell = np.arange(length)
    gap = cell[None, :] - cell[:, None]
    reach = np.abs(gap).astype(np.float64)
    taps = np.where(reach > 0, tail * root**reach, 0.0) - np.where(reach == 1, side, 0.0)
    high, low = split(step_scale * np.sign(gap) * taps)
    return np.concatenate(
        [np.concatenate([high, low], 1), np.concatenate([high, low], 1)], 0
    )


def arrival_rows(length):
    cell = np.arange(length, dtype=np.float64)
    rows = np.zeros((4, length))
    rows[0] = tail * root**cell
    rows[1, 0] = -side
    rows[2] = -tail * root ** (length - 1.0 - cell)
    rows[3, length - 1] = side
    return rows


def stack_arrival(rows):
    length = rows.shape[1]
    stacked = np.zeros((2, 3 * arrival_depth, fields * length), ml_dtypes.bfloat16)
    for place, order in enumerate(((2, 3, 0, 1), (0, 1, 2, 3))):
        high, low = split(rows[list(order)])
        for n in range(4):
            for c in range(fields):
                at = (n // 2) * 2 * fields + 2 * c + n % 2
                lanes = slice(c * length, (c + 1) * length)
                stacked[place, at, lanes] = high[n]
                stacked[place, arrival_depth + at, lanes] = high[n]
                stacked[place, 2 * arrival_depth + at, lanes] = low[n]
    return stacked


def in_hbm(values):
    return pltpu.with_memory_space_constraint(values, pltpu.HBM)


def ends_kernel(
    rows, costate_hbm, weights_hbm, matrix_hbm, arrive_hbm, held, even_x_ref, even_z_ref, odd_z_ref,
    odd_x_ref, matrix_ref, arrive_ref, weights_ref, sems,
):
    per_segment = rows // segments
    place = lax.axis_index("gz") % 2
    constants = [
        pltpu.make_async_copy(source, target, sems.at[fields + n])
        for n, (source, target) in enumerate(
            (
                (weights_hbm.at[place], weights_ref),
                (matrix_hbm, matrix_ref),
                (arrive_hbm.at[place], arrive_ref),
            )
        )
    ]
    constants[0].start()
    for c in range(fields):
        pltpu.make_async_copy(costate_hbm.at[c], held.at[c], sems.at[c]).start()
    constants[1].start()
    constants[2].start()
    x_even = lax.axis_index("gx") % 2 == 0
    constants[0].wait()

    def component(c, carry):
        pltpu.make_async_copy(costate_hbm.at[c], held.at[c], sems.at[c]).wait()
        lines = held[c].reshape(-1, 128)
        high = lines.astype(jnp.bfloat16)
        low = (lines - high.astype(jnp.float32)).astype(jnp.bfloat16)
        sums = lax.dot_general(
            weights_ref[...],
            jnp.concatenate([high, low], 1),
            (((1,), (1,)), ((), ())),
            preferred_element_type=jnp.float32,
        )
        sums = sums[0:8] + sums[8:16]
        even_z_ref[c] = sums[0:2]
        odd_z_ref[c] = sums[2:4]
        ahead = held[c, :, 0]
        back = held[c, :, per_segment - 1]
        for j in range(1, per_segment):
            ahead = ahead * root + held[c, :, j]
            back = back * root + held[c, :, per_segment - 1 - j]
        right = [ahead[segments - 1 - s] * float(root ** (1 + s * per_segment)) for s in range(segments)]
        left = [back[s] * float(root ** (1 + s * per_segment)) for s in range(segments)]
        while len(right) > 1:
            right = [right[n] + right[n + 1] for n in range(0, len(right), 2)]
            left = [left[n] + left[n + 1] for n in range(0, len(left), 2)]
        first = held[c, 0, 0]
        last = held[c, segments - 1, per_segment - 1]
        even_x_ref[c, 0] = jnp.where(x_even, right[0], left[0])
        even_x_ref[c, 1] = jnp.where(x_even, last, first)
        odd_x_ref[c, 0] = jnp.where(x_even, left[0], right[0])
        odd_x_ref[c, 1] = jnp.where(x_even, first, last)
        return carry

    lax.fori_loop(0, fields, component, 0)
    constants[1].wait()
    constants[2].wait()


def pull(a, b, u0, u1, u2, h, k):
    a4u0 = a[4] * u0
    b4u2 = b[4] * u2
    both = a4u0 + b4u2
    g = (gas_gamma - 1.0) * (a[1] + b[3] + both)
    a1u0 = a[1] * u0
    b3u2 = b[3] * u2
    v0 = a1u0 + a[2] * u1 + a[3] * u2 + a[4] * h
    v2 = b[1] * u0 + b[2] * u1 + b3u2 + b[4] * h
    mass = g * k - v0 * u0 - v2 * u2
    m0 = a[0] + a1u0 + b[1] * u2 + v0 - g * u0
    m1 = a[2] * u0 + b[2] * u2 - g * u1
    m2 = b[0] + a[3] * u0 + b3u2 + v2 - g * u2
    energy = both + g
    return [mass, m0, m1, m2, energy]


def slope_body(
    rows, costate_ref, even_x_ref, matrix_ref, density_hbm, momentum_hbm, energy_hbm,
    stream_ref, span_ref, coef_ref, density_ref, momentum_ref, energy_ref, sems,
):
    copies = [
        pltpu.make_async_copy(source, target, sems.at[n])
        for n, (source, target) in enumerate(
            (
                (density_hbm, density_ref),
                (momentum_hbm, momentum_ref),
                (energy_hbm, energy_ref),
            )
        )
    ]
    for copy in copies:
        copy.start()
    x_even = lax.axis_index("gx") % 2 == 0
    gain = step_scale * tail
    edge = step_scale * side
    from_right = jnp.where(x_even, 1.0, 0.0).astype(jnp.float32)
    from_left = 1.0 - from_right
    right_sum = tuple(even_x_ref[c, 0] * (from_right * gain) for c in range(fields))
    for c in range(fields):
        stream_ref[c, rows - 1] = right_sum[c] - even_x_ref[c, 1] * (from_right * edge)

    def backward(step, carry):
        i = rows - 2 - step
        nxt = []
        for c in range(fields):
            after = costate_ref[c, i + 1]
            now = carry[c] * root + after * (gain * root)
            stream_ref[c, i] = now - after * edge
            nxt.append(now)
        return tuple(nxt)

    lax.fori_loop(0, rows - 1, backward, right_sum, unroll=8)

    def across(c, carry):
        lines = costate_ref[c].reshape(-1, 128)
        high = lines.astype(jnp.bfloat16)
        low = (lines - high.astype(jnp.float32)).astype(jnp.bfloat16)
        out = jnp.dot(
            jnp.concatenate([high, low], 1), matrix_ref[...], preferred_element_type=jnp.float32
        )
        span_ref[c] = (out[:, :128] + out[:, 128:]).reshape(rows, 8, 128)
        return carry

    lax.fori_loop(0, fields, across, 0)
    for copy in copies:
        copy.wait()

    def forward(i, carry):
        ahead, before = carry
        rho = density_ref[i]
        inverse = pl.reciprocal(rho, approx=True)
        inverse = inverse * (2.0 - rho * inverse)
        inverse = inverse * (2.0 - rho * inverse)
        u0 = momentum_ref[0, i] * inverse
        u1 = momentum_ref[1, i] * inverse
        u2 = momentum_ref[2, i] * inverse
        k = 0.5 * (u0 * u0 + u1 * u1 + u2 * u2)
        h = gas_gamma * (energy_ref[i] * inverse) - (gas_gamma - 1.0) * k
        for slot, value in enumerate((u0, u1, u2, h, k)):
            coef_ref[slot, i] = value
        ahead = tuple(ahead[c] * root + before[c] * (gain * root) for c in range(fields))
        for c in range(fields):
            stream_ref[c, i] = ahead[c] - before[c] * edge - stream_ref[c, i]
        return ahead, tuple(costate_ref[c, i] for c in range(fields))

    before = tuple(even_x_ref[c, 1] * from_left for c in range(fields))
    ahead = tuple(
        (even_x_ref[c, 0] * (from_left / root) - before[c]) * gain for c in range(fields)
    )
    lax.fori_loop(0, rows, forward, (ahead, before), unroll=4)


def early_slope_kernel(rows, *refs):
    odd_x_in, refs = refs[6], refs[:6] + refs[7:]
    odd_x_out, refs = refs[9], refs[:9] + refs[10:]

    @pl.when(lax.axis_index("gx") == 0)
    def _():
        slope_body(rows, *refs)


def late_slope_kernel(rows, *refs):
    refs = refs[:6] + refs[9:]

    @pl.when(lax.axis_index("gx") != 0)
    def _():
        slope_body(rows, *refs)


def gather_kernel(
    rows, costate_ref, stream_ref, span_ref, coef_ref, even_z_ref, odd_z_ref, arrive_ref,
    partial_ref, values, arrived,
):
    count = 2 * fields
    half = rows // 2
    width = half * 8
    values[16:24] = jnp.zeros((8, values.shape[1]), jnp.float32)
    for c in range(fields):
        values[2 * c : 2 * c + 2] = even_z_ref[c]
        values[count + 2 * c : count + 2 * c + 2] = odd_z_ref[c]
    for part in range(2):
        whole = values[:, part * width : (part + 1) * width]
        top = whole.astype(jnp.bfloat16).astype(jnp.float32)
        stacked = jnp.concatenate([top, whole - top, top], 0)
        columns = jnp.swapaxes(stacked, 0, 1).astype(jnp.bfloat16)
        out = jnp.dot(columns, arrive_ref[...], preferred_element_type=jnp.float32)
        for c in range(fields):
            arrived[c, part * half : (part + 1) * half] = out[:, c * 128 : (c + 1) * 128].reshape(
                half, 8, 128
            )

    def add(i, carry):
        a = [stream_ref[c, i] for c in range(fields)]
        b = [span_ref[c, i] + arrived[c, i] for c in range(fields)]
        pulled = pull(a, b, *[coef_ref[slot, i] for slot in range(5)])
        for c in range(fields):
            partial_ref[c, i] = costate_ref[c, i] + pulled[c]
        return carry

    lax.fori_loop(0, rows, add, 0, unroll=4)


def pull_stream(a, u0, u1, u2, h, k):
    both = a[4] * u0
    g = (gas_gamma - 1.0) * (a[1] + both)
    a1u0 = a[1] * u0
    v0 = a1u0 + a[2] * u1 + a[3] * u2 + a[4] * h
    return [
        g * k - v0 * u0,
        a[0] + a1u0 + v0 - g * u0,
        a[2] * u0 - g * u1,
        a[3] * u0 - g * u2,
        both + g,
    ]


def join_kernel(rows, partial_ref, coef_ref, odd_x_ref, out_hbm, result, sems):
    place = lax.axis_index("gx") % 2
    per_segment = rows // segments
    sign = jnp.where(place == 0, 1.0, -1.0).astype(jnp.float32)

    def copy_out(s):
        at = jnp.where(place == 0, s, segments - 1 - s)
        part = pl.ds(at * per_segment, per_segment)
        return pltpu.make_async_copy(result.at[:, part], out_hbm.at[:, part], sems.at[s])

    def step(t, a):
        i = jnp.where(place == 0, t, rows - 1 - t)
        pulled = pull_stream(a, *[coef_ref[slot, i] for slot in range(5)])
        for c in range(fields):
            result[c, i] = partial_ref[c, i] + pulled[c]

    def segment(s, carry):
        for j in range(per_segment):
            now = carry
            if j == 0:
                edge = jnp.where(s == 0, -sign * (step_scale * side), 0.0).astype(jnp.float32)
                now = tuple(carry[c] + edge * odd_x_ref[c, 1] for c in range(fields))
            step(s * per_segment + j, now)
            carry = tuple(value * root for value in carry)
        copy_out(s).start()
        return carry

    total = tuple(odd_x_ref[c, 0] * (sign * (step_scale * tail)) for c in range(fields))
    lax.fori_loop(0, segments, segment, total)

    def finish(s, carry):
        copy_out(s).wait()
        return carry

    lax.fori_loop(0, segments, finish, 0)


def per_device(density, momentum, energy, costate):
    rows, planes, cells = density.shape
    f32 = jnp.float32
    whole = pl.BlockSpec(memory_space=pltpu.VMEM)
    hbm = pl.BlockSpec(memory_space=pltpu.HBM)
    params = pltpu.CompilerParams(vmem_limit_bytes=vmem_bytes)
    x_shape = jax.ShapeDtypeStruct((fields, 2, planes, cells), f32)
    z_shape = jax.ShapeDtypeStruct((fields, 2, rows * planes), f32)
    block = jax.ShapeDtypeStruct((fields, rows, planes, cells), f32)
    per_segment = rows // segments

    matrix = local_matrix(cells)
    arrive = stack_arrival(step_scale * arrival_rows(cells))
    held, even_x, even_z, odd_z, odd_x, matrix, arrive = pl.pallas_call(
        lambda *refs: ends_kernel(rows, *refs),
        out_shape=(
            jax.ShapeDtypeStruct((fields, segments, per_segment, planes, cells), f32),
            x_shape,
            z_shape,
            z_shape,
            x_shape,
            jax.ShapeDtypeStruct(matrix.shape, jnp.bfloat16),
            jax.ShapeDtypeStruct(arrive.shape[1:], jnp.bfloat16),
        ),
        in_specs=[hbm] * 4,
        out_specs=(whole,) * 7,
        scratch_shapes=[
            pltpu.VMEM((16, 2 * cells), jnp.bfloat16),
            pltpu.SemaphoreType.DMA((fields + 3,)),
        ],
        compiler_params=params,
        name="ends",
    )(
        in_hbm(costate.reshape(fields, segments, per_segment, planes, cells)),
        in_hbm(jnp.asarray(stack_ends(end_weights(cells)))),
        in_hbm(jnp.asarray(matrix)),
        in_hbm(jnp.asarray(arrive)),
    )
    held = held.reshape(costate.shape)

    def pairs(values, axis, odd):
        count = lax.axis_size(axis)
        links = []
        for i in range(odd, count + odd, 2):
            a, b = i % count, (i + 1) % count
            links += [(a, b), (b, a)]
        return lax.ppermute(values, axis, links)

    even_x = pairs(even_x, "gx", 0)
    even_z = pairs(even_z, "gz", 0)
    odd_z = pairs(odd_z, "gz", 1)

    state = (
        pltpu.VMEM((rows, planes, cells), f32),
        pltpu.VMEM((3, rows, planes, cells), f32),
        pltpu.VMEM((rows, planes, cells), f32),
    )
    inputs = (held, even_x, matrix, in_hbm(density), in_hbm(momentum), in_hbm(energy))
    stream, span, coef, odd_x = pl.pallas_call(
        lambda *refs: early_slope_kernel(rows, *refs),
        out_shape=(block, block, block, x_shape),
        in_specs=[whole] * 3 + [hbm] * 3 + [whole],
        out_specs=(whole,) * 4,
        scratch_shapes=[*state, pltpu.SemaphoreType.DMA((3,))],
        input_output_aliases={6: 3},
        compiler_params=params,
        name="early_slope",
    )(*inputs, odd_x)

    odd_x = pairs(odd_x, "gx", 1)

    stream, span, coef = pl.pallas_call(
        lambda *refs: late_slope_kernel(rows, *refs),
        out_shape=(block,) * 3,
        in_specs=[whole] * 3 + [hbm] * 3 + [whole] * 3,
        out_specs=(whole,) * 3,
        scratch_shapes=[*state, pltpu.SemaphoreType.DMA((3,))],
        input_output_aliases={6: 0, 7: 1, 8: 2},
        compiler_params=params,
        cost_estimate=pl.CostEstimate(flops=300_000_000, bytes_accessed=10_000_000, transcendentals=0),
        name="late_slope",
    )(*inputs, stream, span, coef)

    partial = pl.pallas_call(
        lambda *refs: gather_kernel(rows, *refs),
        out_shape=block,
        in_specs=[whole] * 7,
        out_specs=whole,
        scratch_shapes=[
            pltpu.VMEM((arrival_depth, rows * planes), f32),
            pltpu.VMEM((fields, rows, planes, cells), f32),
        ],
        compiler_params=params,
        cost_estimate=pl.CostEstimate(flops=100_000_000, bytes_accessed=10_000_000, transcendentals=0),
        name="gather",
    )(held, stream, span, coef, even_z, odd_z, arrive)

    return pl.pallas_call(
        lambda *refs: join_kernel(rows, *refs),
        out_shape=block,
        in_specs=[whole] * 3,
        out_specs=hbm,
        scratch_shapes=[
            pltpu.VMEM((fields, rows, planes, cells), f32),
            pltpu.SemaphoreType.DMA((segments,)),
        ],
        compiler_params=params,
        name="join",
    )(partial, coef, odd_x)


def solution(mesh):
    return jax.shard_map(
        per_device,
        mesh=mesh,
        in_specs=(
            P("gx", None, "gz"),
            P(None, "gx", None, "gz"),
            P("gx", None, "gz"),
            P(None, "gx", None, "gz"),
        ),
        out_specs=P(None, "gx", None, "gz"),
        check_vma=False,
    )
```

```python
import math

import jax
import jax.numpy as jnp
import ml_dtypes
import numpy as np
from jax import lax
from jax.experimental import pallas as pl
from jax.experimental.pallas import tpu as pltpu
from jax.sharding import PartitionSpec as P

pade_alpha = 1.0 / 3.0
near_coef = 14.0 / 9.0
far_coef = 1.0 / 9.0
step_scale = 0.1
gas_gamma = 1.4

root = (-1.0 + math.sqrt(1.0 - 4.0 * pade_alpha * pade_alpha)) / (2.0 * pade_alpha)
side = 0.25 * far_coef / pade_alpha
tail = (0.5 * near_coef - side) / pade_alpha

fields = 5
segments = 8
arrival_depth = 24
vmem_bytes = 16 * 1024 * 1024


def split(values):
    high = values.astype(ml_dtypes.bfloat16)
    low = (values - high.astype(np.float64)).astype(ml_dtypes.bfloat16)
    return high, low


def end_weights(length):
    cell = np.arange(length, dtype=np.float64)
    rows = np.zeros((4, length))
    rows[0] = root ** (length - cell)
    rows[1, length - 1] = 1.0
    rows[2] = root ** (cell + 1.0)
    rows[3, 0] = 1.0
    return rows


def stack_ends(rows):
    stacked = np.zeros((2, 16, 2 * rows.shape[1]), ml_dtypes.bfloat16)
    for place, order in enumerate(((0, 1, 2, 3), (2, 3, 0, 1))):
        high, low = split(rows[list(order)])
        stacked[place, 0:4] = np.concatenate([high, high], 1)
        stacked[place, 8:12] = np.concatenate([low, np.zeros_like(low)], 1)
    return stacked


def local_matrix(length):
    cell = np.arange(length)
    gap = cell[None, :] - cell[:, None]
    reach = np.abs(gap).astype(np.float64)
    taps = np.where(reach > 0, tail * root**reach, 0.0) - np.where(reach == 1, side, 0.0)
    high, low = split(step_scale * np.sign(gap) * taps)
    return np.concatenate(
        [np.concatenate([high, low], 1), np.concatenate([high, low], 1)], 0
    )


def arrival_rows(length):
    cell = np.arange(length, dtype=np.float64)
    rows = np.zeros((4, length))
    rows[0] = tail * root**cell
    rows[1, 0] = -side
    rows[2] = -tail * root ** (length - 1.0 - cell)
    rows[3, length - 1] = side
    return rows


def stack_arrival(rows):
    length = rows.shape[1]
    stacked = np.zeros((2, 3 * arrival_depth, fields * length), ml_dtypes.bfloat16)
    for place, order in enumerate(((2, 3, 0, 1), (0, 1, 2, 3))):
        high, low = split(rows[list(order)])
        for n in range(4):
            for c in range(fields):
                at = (n // 2) * 2 * fields + 2 * c + n % 2
                lanes = slice(c * length, (c + 1) * length)
                stacked[place, at, lanes] = high[n]
                stacked[place, arrival_depth + at, lanes] = high[n]
                stacked[place, 2 * arrival_depth + at, lanes] = low[n]
    return stacked


def in_hbm(values):
    return pltpu.with_memory_space_constraint(values, pltpu.HBM)


def ends_kernel(
    rows, costate_hbm, weights_hbm, matrix_hbm, arrive_hbm, held, even_x_ref, even_z_ref, odd_z_ref,
    odd_x_ref, matrix_ref, arrive_ref, weights_ref, sems,
):
    per_segment = rows // segments
    place = lax.axis_index("gz") % 2
    constants = [
        pltpu.make_async_copy(source, target, sems.at[fields + n])
        for n, (source, target) in enumerate(
            (
                (weights_hbm.at[place], weights_ref),
                (matrix_hbm, matrix_ref),
                (arrive_hbm.at[place], arrive_ref),
            )
        )
    ]
    constants[0].start()
    for c in range(fields):
        pltpu.make_async_copy(costate_hbm.at[c], held.at[c], sems.at[c]).start()
    constants[1].start()
    constants[2].start()
    x_even = lax.axis_index("gx") % 2 == 0
    constants[0].wait()

    def component(c, carry):
        pltpu.make_async_copy(costate_hbm.at[c], held.at[c], sems.at[c]).wait()
        lines = held[c].reshape(-1, 128)
        high = lines.astype(jnp.bfloat16)
        low = (lines - high.astype(jnp.float32)).astype(jnp.bfloat16)
        sums = lax.dot_general(
            weights_ref[...],
            jnp.concatenate([high, low], 1),
            (((1,), (1,)), ((), ())),
            preferred_element_type=jnp.float32,
        )
        sums = sums[0:8] + sums[8:16]
        even_z_ref[c] = sums[0:2]
        odd_z_ref[c] = sums[2:4]
        ahead = held[c, :, 0]
        back = held[c, :, per_segment - 1]
        for j in range(1, per_segment):
            ahead = ahead * root + held[c, :, j]
            back = back * root + held[c, :, per_segment - 1 - j]
        right = [ahead[segments - 1 - s] * float(root ** (1 + s * per_segment)) for s in range(segments)]
        left = [back[s] * float(root ** (1 + s * per_segment)) for s in range(segments)]
        while len(right) > 1:
            right = [right[n] + right[n + 1] for n in range(0, len(right), 2)]
            left = [left[n] + left[n + 1] for n in range(0, len(left), 2)]
        first = held[c, 0, 0]
        last = held[c, segments - 1, per_segment - 1]
        even_x_ref[c, 0] = jnp.where(x_even, right[0], left[0])
        even_x_ref[c, 1] = jnp.where(x_even, last, first)
        odd_x_ref[c, 0] = jnp.where(x_even, left[0], right[0])
        odd_x_ref[c, 1] = jnp.where(x_even, first, last)
        return carry

    lax.fori_loop(0, fields, component, 0)
    constants[1].wait()
    constants[2].wait()


def pull(a, b, u0, u1, u2, h, k):
    a4u0 = a[4] * u0
    b4u2 = b[4] * u2
    both = a4u0 + b4u2
    g = (gas_gamma - 1.0) * (a[1] + b[3] + both)
    a1u0 = a[1] * u0
    b3u2 = b[3] * u2
    v0 = a1u0 + a[2] * u1 + a[3] * u2 + a[4] * h
    v2 = b[1] * u0 + b[2] * u1 + b3u2 + b[4] * h
    mass = g * k - v0 * u0 - v2 * u2
    m0 = a[0] + a1u0 + b[1] * u2 + v0 - g * u0
    m1 = a[2] * u0 + b[2] * u2 - g * u1
    m2 = b[0] + a[3] * u0 + b3u2 + v2 - g * u2
    energy = both + g
    return [mass, m0, m1, m2, energy]


def slope_body(
    rows, costate_ref, even_x_ref, matrix_ref, density_hbm, momentum_hbm, energy_hbm,
    stream_ref, span_ref, coef_ref, density_ref, momentum_ref, energy_ref, sems,
):
    copies = [
        pltpu.make_async_copy(source, target, sems.at[n])
        for n, (source, target) in enumerate(
            (
                (density_hbm, density_ref),
                (momentum_hbm, momentum_ref),
                (energy_hbm, energy_ref),
            )
        )
    ]
    for copy in copies:
        copy.start()
    x_even = lax.axis_index("gx") % 2 == 0
    gain = step_scale * tail
    edge = step_scale * side
    from_right = jnp.where(x_even, 1.0, 0.0).astype(jnp.float32)
    from_left = 1.0 - from_right
    right_sum = tuple(even_x_ref[c, 0] * (from_right * gain) for c in range(fields))
    for c in range(fields):
        stream_ref[c, rows - 1] = right_sum[c] - even_x_ref[c, 1] * (from_right * edge)

    def backward(step, carry):
        i = rows - 2 - step
        nxt = []
        for c in range(fields):
            after = costate_ref[c, i + 1]
            now = carry[c] * root + after * (gain * root)
            stream_ref[c, i] = now - after * edge
            nxt.append(now)
        return tuple(nxt)

    lax.fori_loop(0, rows - 1, backward, right_sum, unroll=8)

    def across(c, carry):
        lines = costate_ref[...].reshape(-1, 128)
        high = lines.astype(jnp.bfloat16)
        low = (lines - high.astype(jnp.float32)).astype(jnp.bfloat16)
        out = jnp.dot(
            jnp.concatenate([high, low], 1), matrix_ref[...], preferred_element_type=jnp.float32
        )
        span_ref[...] = (out[:, :128] + out[:, 128:]).reshape(fields, rows, 8, 128)
        return carry

    across(0, 0)
    def forward(i, carry):
        ahead, before = carry
        ahead = tuple(ahead[c] * root + before[c] * (gain * root) for c in range(fields))
        for c in range(fields):
            stream_ref[c, i] = ahead[c] - before[c] * edge - stream_ref[c, i]
        return ahead, tuple(costate_ref[c, i] for c in range(fields))

    before = tuple(even_x_ref[c, 1] * from_left for c in range(fields))
    ahead = tuple(
        (even_x_ref[c, 0] * (from_left / root) - before[c]) * gain for c in range(fields)
    )
    lax.fori_loop(0, rows, forward, (ahead, before), unroll=8)
    for copy in copies:
        copy.wait()

    def state(i, carry):
        rho = density_ref[i]
        inverse = pl.reciprocal(rho, approx=True)
        inverse = inverse * (2.0 - rho * inverse)
        u0 = momentum_ref[0, i] * inverse
        u1 = momentum_ref[1, i] * inverse
        u2 = momentum_ref[2, i] * inverse
        k = 0.5 * (u0 * u0 + u1 * u1 + u2 * u2)
        h = gas_gamma * (energy_ref[i] * inverse) - (gas_gamma - 1.0) * k
        for slot, value in enumerate((u0, u1, u2, h, k)):
            coef_ref[slot, i] = value
        return carry

    lax.fori_loop(0, rows, state, 0, unroll=8)


def early_slope_kernel(rows, *refs):
    odd_x_in, refs = refs[6], refs[:6] + refs[7:]
    odd_x_out, refs = refs[9], refs[:9] + refs[10:]

    @pl.when(lax.axis_index("gx") == 0)
    def _():
        slope_body(rows, *refs)


def late_slope_kernel(rows, *refs):
    refs = refs[:6] + refs[9:]

    @pl.when(lax.axis_index("gx") != 0)
    def _():
        slope_body(rows, *refs)


def gather_kernel(
    rows, costate_ref, stream_ref, span_ref, coef_ref, even_z_ref, odd_z_ref, arrive_ref,
    partial_ref, values, arrived,
):
    count = 2 * fields
    half = rows // 2
    width = half * 8
    values[16:24] = jnp.zeros((8, values.shape[1]), jnp.float32)
    for c in range(fields):
        values[2 * c : 2 * c + 2] = even_z_ref[c]
        values[count + 2 * c : count + 2 * c + 2] = odd_z_ref[c]
    for part in range(2):
        whole = values[:, part * width : (part + 1) * width]
        top = whole.astype(jnp.bfloat16).astype(jnp.float32)
        stacked = jnp.concatenate([top, whole - top, top], 0)
        columns = jnp.swapaxes(stacked, 0, 1).astype(jnp.bfloat16)
        out = jnp.dot(columns, arrive_ref[...], preferred_element_type=jnp.float32)
        for c in range(fields):
            arrived[c, part * half : (part + 1) * half] = out[:, c * 128 : (c + 1) * 128].reshape(
                half, 8, 128
            )

    def add(i, carry):
        a = [stream_ref[c, i] for c in range(fields)]
        b = [span_ref[c, i] + arrived[c, i] for c in range(fields)]
        pulled = pull(a, b, *[coef_ref[slot, i] for slot in range(5)])
        for c in range(fields):
            partial_ref[c, i] = costate_ref[c, i] + pulled[c]
        return carry

    lax.fori_loop(0, rows, add, 0, unroll=8)


def pull_stream(a, u0, u1, u2, h, k):
    both = a[4] * u0
    g = (gas_gamma - 1.0) * (a[1] + both)
    a1u0 = a[1] * u0
    v0 = a1u0 + a[2] * u1 + a[3] * u2 + a[4] * h
    return [
        g * k - v0 * u0,
        a[0] + a1u0 + v0 - g * u0,
        a[2] * u0 - g * u1,
        a[3] * u0 - g * u2,
        both + g,
    ]


def join_kernel(rows, partial_ref, coef_ref, odd_x_ref, out_hbm, result, sems):
    place = lax.axis_index("gx") % 2
    per_segment = rows // segments
    sign = jnp.where(place == 0, 1.0, -1.0).astype(jnp.float32)

    def copy_out(s):
        at = jnp.where(place == 0, s, segments - 1 - s)
        part = pl.ds(at * per_segment, per_segment)
        return pltpu.make_async_copy(result.at[:, part], out_hbm.at[:, part], sems.at[s])

    def step(t, a):
        i = jnp.where(place == 0, t, rows - 1 - t)
        pulled = pull_stream(a, *[coef_ref[slot, i] for slot in range(5)])
        for c in range(fields):
            result[c, i] = partial_ref[c, i] + pulled[c]

    def segment(s, carry):
        for j in range(per_segment):
            now = carry
            if j == 0:
                edge = jnp.where(s == 0, -sign * (step_scale * side), 0.0).astype(jnp.float32)
                now = tuple(carry[c] + edge * odd_x_ref[c, 1] for c in range(fields))
            step(s * per_segment + j, now)
            carry = tuple(value * root for value in carry)
        copy_out(s).start()
        return carry

    total = tuple(odd_x_ref[c, 0] * (sign * (step_scale * tail)) for c in range(fields))
    lax.fori_loop(0, segments, segment, total)

    def finish(s, carry):
        copy_out(s).wait()
        return carry

    lax.fori_loop(0, segments, finish, 0)


def per_device(density, momentum, energy, costate):
    rows, planes, cells = density.shape
    f32 = jnp.float32
    whole = pl.BlockSpec(memory_space=pltpu.VMEM)
    hbm = pl.BlockSpec(memory_space=pltpu.HBM)
    params = pltpu.CompilerParams(vmem_limit_bytes=vmem_bytes)
    x_shape = jax.ShapeDtypeStruct((fields, 2, planes, cells), f32)
    z_shape = jax.ShapeDtypeStruct((fields, 2, rows * planes), f32)
    block = jax.ShapeDtypeStruct((fields, rows, planes, cells), f32)
    per_segment = rows // segments

    matrix = local_matrix(cells)
    arrive = stack_arrival(step_scale * arrival_rows(cells))
    held, even_x, even_z, odd_z, odd_x, matrix, arrive = pl.pallas_call(
        lambda *refs: ends_kernel(rows, *refs),
        out_shape=(
            jax.ShapeDtypeStruct((fields, segments, per_segment, planes, cells), f32),
            x_shape,
            z_shape,
            z_shape,
            x_shape,
            jax.ShapeDtypeStruct(matrix.shape, jnp.bfloat16),
            jax.ShapeDtypeStruct(arrive.shape[1:], jnp.bfloat16),
        ),
        in_specs=[hbm] * 4,
        out_specs=(whole,) * 7,
        scratch_shapes=[
            pltpu.VMEM((16, 2 * cells), jnp.bfloat16),
            pltpu.SemaphoreType.DMA((fields + 3,)),
        ],
        compiler_params=params,
        name="ends",
    )(
        in_hbm(costate.reshape(fields, segments, per_segment, planes, cells)),
        in_hbm(jnp.asarray(stack_ends(end_weights(cells)))),
        in_hbm(jnp.asarray(matrix)),
        in_hbm(jnp.asarray(arrive)),
    )
    held = held.reshape(costate.shape)

    def pairs(values, axis, odd):
        count = lax.axis_size(axis)
        links = []
        for i in range(odd, count + odd, 2):
            a, b = i % count, (i + 1) % count
            links += [(a, b), (b, a)]
        return lax.ppermute(values, axis, links)

    even_x = pairs(even_x, "gx", 0)
    even_z = pairs(even_z, "gz", 0)
    odd_z = pairs(odd_z, "gz", 1)

    state = (
        pltpu.VMEM((rows, planes, cells), f32),
        pltpu.VMEM((3, rows, planes, cells), f32),
        pltpu.VMEM((rows, planes, cells), f32),
    )
    inputs = (held, even_x, matrix, in_hbm(density), in_hbm(momentum), in_hbm(energy))
    stream, span, coef, odd_x = pl.pallas_call(
        lambda *refs: early_slope_kernel(rows, *refs),
        out_shape=(block, block, block, x_shape),
        in_specs=[whole] * 3 + [hbm] * 3 + [whole],
        out_specs=(whole,) * 4,
        scratch_shapes=[*state, pltpu.SemaphoreType.DMA((3,))],
        input_output_aliases={6: 3},
        compiler_params=params,
        name="early_slope",
    )(*inputs, odd_x)

    odd_x = pairs(odd_x, "gx", 1)

    stream, span, coef = pl.pallas_call(
        lambda *refs: late_slope_kernel(rows, *refs),
        out_shape=(block,) * 3,
        in_specs=[whole] * 3 + [hbm] * 3 + [whole] * 3,
        out_specs=(whole,) * 3,
        scratch_shapes=[*state, pltpu.SemaphoreType.DMA((3,))],
        input_output_aliases={6: 0, 7: 1, 8: 2},
        compiler_params=params,
        cost_estimate=pl.CostEstimate(flops=300_000_000, bytes_accessed=10_000_000, transcendentals=0),
        name="late_slope",
    )(*inputs, stream, span, coef)

    partial = pl.pallas_call(
        lambda *refs: gather_kernel(rows, *refs),
        out_shape=block,
        in_specs=[whole] * 7,
        out_specs=whole,
        scratch_shapes=[
            pltpu.VMEM((arrival_depth, rows * planes), f32),
            pltpu.VMEM((fields, rows, planes, cells), f32),
        ],
        compiler_params=params,
        cost_estimate=pl.CostEstimate(flops=100_000_000, bytes_accessed=10_000_000, transcendentals=0),
        name="gather",
    )(held, stream, span, coef, even_z, odd_z, arrive)

    return pl.pallas_call(
        lambda *refs: join_kernel(rows, *refs),
        out_shape=block,
        in_specs=[whole] * 3,
        out_specs=hbm,
        scratch_shapes=[
            pltpu.VMEM((fields, rows, planes, cells), f32),
            pltpu.SemaphoreType.DMA((segments,)),
        ],
        compiler_params=params,
        name="join",
    )(partial, coef, odd_x)


def solution(mesh):
    return jax.shard_map(
        per_device,
        mesh=mesh,
        in_specs=(
            P("gx", None, "gz"),
            P(None, "gx", None, "gz"),
            P("gx", None, "gz"),
            P(None, "gx", None, "gz"),
        ),
        out_specs=P(None, "gx", None, "gz"),
        check_vma=False,
    )
```

```python
import math

import jax
import jax.numpy as jnp
import ml_dtypes
import numpy as np
from jax import lax
from jax.experimental import pallas as pl
from jax.experimental.pallas import tpu as pltpu
from jax.sharding import PartitionSpec as P

pade_alpha = 1.0 / 3.0
near_coef = 14.0 / 9.0
far_coef = 1.0 / 9.0
step_scale = 0.1
gas_gamma = 1.4

root = (-1.0 + math.sqrt(1.0 - 4.0 * pade_alpha * pade_alpha)) / (2.0 * pade_alpha)
side = 0.25 * far_coef / pade_alpha
tail = (0.5 * near_coef - side) / pade_alpha

fields = 5
segments = 8
pieces = 16
arrival_depth = 24
vmem_bytes = 16 * 1024 * 1024


def split(values):
    high = values.astype(ml_dtypes.bfloat16)
    low = (values - high.astype(np.float64)).astype(ml_dtypes.bfloat16)
    return high, low


def end_weights(length):
    cell = np.arange(length, dtype=np.float64)
    rows = np.zeros((4, length))
    rows[0] = root ** (length - cell)
    rows[1, length - 1] = 1.0
    rows[2] = root ** (cell + 1.0)
    rows[3, 0] = 1.0
    return rows


def stack_ends(rows):
    stacked = np.zeros((2, 16, 2 * rows.shape[1]), ml_dtypes.bfloat16)
    for place, order in enumerate(((0, 1, 2, 3), (2, 3, 0, 1))):
        high, low = split(rows[list(order)])
        stacked[place, 0:4] = np.concatenate([high, high], 1)
        stacked[place, 8:12] = np.concatenate([low, np.zeros_like(low)], 1)
    return stacked


def local_matrix(length):
    cell = np.arange(length)
    gap = cell[None, :] - cell[:, None]
    reach = np.abs(gap).astype(np.float64)
    taps = np.where(reach > 0, tail * root**reach, 0.0) - np.where(reach == 1, side, 0.0)
    high, low = split(step_scale * np.sign(gap) * taps)
    return np.concatenate(
        [np.concatenate([high, low], 1), np.concatenate([high, low], 1)], 0
    )


def arrival_rows(length):
    cell = np.arange(length, dtype=np.float64)
    rows = np.zeros((4, length))
    rows[0] = tail * root**cell
    rows[1, 0] = -side
    rows[2] = -tail * root ** (length - 1.0 - cell)
    rows[3, length - 1] = side
    return rows


def stack_arrival(rows):
    length = rows.shape[1]
    stacked = np.zeros((2, 3 * arrival_depth, fields * length), ml_dtypes.bfloat16)
    for place, order in enumerate(((2, 3, 0, 1), (0, 1, 2, 3))):
        high, low = split(rows[list(order)])
        for n in range(4):
            for c in range(fields):
                at = (n // 2) * 2 * fields + 2 * c + n % 2
                lanes = slice(c * length, (c + 1) * length)
                stacked[place, at, lanes] = high[n]
                stacked[place, arrival_depth + at, lanes] = high[n]
                stacked[place, 2 * arrival_depth + at, lanes] = low[n]
    return stacked


def in_hbm(values):
    return pltpu.with_memory_space_constraint(values, pltpu.HBM)


def ends_kernel(
    rows, costate_hbm, weights_hbm, matrix_hbm, arrive_hbm, held, even_x_ref, even_z_ref, odd_z_ref,
    odd_x_ref, matrix_ref, arrive_ref, weights_ref, sems,
):
    per_segment = rows // segments
    place = lax.axis_index("gz") % 2
    constants = [
        pltpu.make_async_copy(source, target, sems.at[fields + n])
        for n, (source, target) in enumerate(
            (
                (weights_hbm.at[place], weights_ref),
                (matrix_hbm, matrix_ref),
                (arrive_hbm.at[place], arrive_ref),
            )
        )
    ]
    constants[0].start()
    for c in range(fields):
        pltpu.make_async_copy(costate_hbm.at[c], held.at[c], sems.at[c]).start()
    constants[1].start()
    constants[2].start()
    x_even = lax.axis_index("gx") % 2 == 0
    constants[0].wait()

    def component(c, carry):
        pltpu.make_async_copy(costate_hbm.at[c], held.at[c], sems.at[c]).wait()
        lines = held[c].reshape(-1, 128)
        high = lines.astype(jnp.bfloat16)
        low = (lines - high.astype(jnp.float32)).astype(jnp.bfloat16)
        sums = lax.dot_general(
            weights_ref[...],
            jnp.concatenate([high, low], 1),
            (((1,), (1,)), ((), ())),
            preferred_element_type=jnp.float32,
        )
        sums = sums[0:8] + sums[8:16]
        even_z_ref[c] = sums[0:2]
        odd_z_ref[c] = sums[2:4]
        ahead = held[c, :, 0]
        back = held[c, :, per_segment - 1]
        for j in range(1, per_segment):
            ahead = ahead * root + held[c, :, j]
            back = back * root + held[c, :, per_segment - 1 - j]
        right = [ahead[segments - 1 - s] * float(root ** (1 + s * per_segment)) for s in range(segments)]
        left = [back[s] * float(root ** (1 + s * per_segment)) for s in range(segments)]
        while len(right) > 1:
            right = [right[n] + right[n + 1] for n in range(0, len(right), 2)]
            left = [left[n] + left[n + 1] for n in range(0, len(left), 2)]
        first = held[c, 0, 0]
        last = held[c, segments - 1, per_segment - 1]
        even_x_ref[c, 0] = jnp.where(x_even, right[0], left[0])
        even_x_ref[c, 1] = jnp.where(x_even, last, first)
        odd_x_ref[c, 0] = jnp.where(x_even, left[0], right[0])
        odd_x_ref[c, 1] = jnp.where(x_even, first, last)
        return carry

    lax.fori_loop(0, fields, component, 0)
    constants[1].wait()
    constants[2].wait()


def pull(a, b, u0, u1, u2, h, k):
    a4u0 = a[4] * u0
    b4u2 = b[4] * u2
    both = a4u0 + b4u2
    g = (gas_gamma - 1.0) * (a[1] + b[3] + both)
    a1u0 = a[1] * u0
    b3u2 = b[3] * u2
    v0 = a1u0 + a[2] * u1 + a[3] * u2 + a[4] * h
    v2 = b[1] * u0 + b[2] * u1 + b3u2 + b[4] * h
    mass = g * k - v0 * u0 - v2 * u2
    m0 = a[0] + a1u0 + b[1] * u2 + v0 - g * u0
    m1 = a[2] * u0 + b[2] * u2 - g * u1
    m2 = b[0] + a[3] * u0 + b3u2 + v2 - g * u2
    energy = both + g
    return [mass, m0, m1, m2, energy]


def slope_body(
    rows, costate_ref, even_x_ref, matrix_ref, density_hbm, momentum_hbm, energy_hbm,
    stream_ref, span_ref, coef_ref, density_ref, momentum_ref, energy_ref, sems,
):
    copies = [
        pltpu.make_async_copy(source, target, sems.at[n])
        for n, (source, target) in enumerate(
            (
                (density_hbm, density_ref),
                (momentum_hbm, momentum_ref),
                (energy_hbm, energy_ref),
            )
        )
    ]
    for copy in copies:
        copy.start()
    x_even = lax.axis_index("gx") % 2 == 0
    gain = step_scale * tail
    edge = step_scale * side
    from_right = jnp.where(x_even, 1.0, 0.0).astype(jnp.float32)
    from_left = 1.0 - from_right
    right_sum = tuple(even_x_ref[c, 0] * (from_right * gain) for c in range(fields))
    for c in range(fields):
        stream_ref[c, rows - 1] = right_sum[c] - even_x_ref[c, 1] * (from_right * edge)

    def backward(step, carry):
        i = rows - 2 - step
        nxt = []
        for c in range(fields):
            after = costate_ref[c, i + 1]
            now = carry[c] * root + after * (gain * root)
            stream_ref[c, i] = now - after * edge
            nxt.append(now)
        return tuple(nxt)

    lax.fori_loop(0, rows - 1, backward, right_sum, unroll=8)

    def across(c, carry):
        lines = costate_ref[...].reshape(-1, 128)
        high = lines.astype(jnp.bfloat16)
        low = (lines - high.astype(jnp.float32)).astype(jnp.bfloat16)
        out = jnp.dot(
            jnp.concatenate([high, low], 1), matrix_ref[...], preferred_element_type=jnp.float32
        )
        span_ref[...] = (out[:, :128] + out[:, 128:]).reshape(fields, rows, 8, 128)
        return carry

    across(0, 0)
    def forward(i, carry):
        ahead, before = carry
        ahead = tuple(ahead[c] * root + before[c] * (gain * root) for c in range(fields))
        for c in range(fields):
            stream_ref[c, i] = ahead[c] - before[c] * edge - stream_ref[c, i]
        return ahead, tuple(costate_ref[c, i] for c in range(fields))

    before = tuple(even_x_ref[c, 1] * from_left for c in range(fields))
    ahead = tuple(
        (even_x_ref[c, 0] * (from_left / root) - before[c]) * gain for c in range(fields)
    )
    lax.fori_loop(0, rows, forward, (ahead, before), unroll=8)
    for copy in copies:
        copy.wait()

    def state(i, carry):
        rho = density_ref[i]
        inverse = pl.reciprocal(rho, approx=True)
        inverse = inverse * (2.0 - rho * inverse)
        u0 = momentum_ref[0, i] * inverse
        u1 = momentum_ref[1, i] * inverse
        u2 = momentum_ref[2, i] * inverse
        k = 0.5 * (u0 * u0 + u1 * u1 + u2 * u2)
        h = gas_gamma * (energy_ref[i] * inverse) - (gas_gamma - 1.0) * k
        for slot, value in enumerate((u0, u1, u2, h, k)):
            coef_ref[slot, i] = value
        return carry

    lax.fori_loop(0, rows, state, 0, unroll=16)


def early_slope_kernel(rows, *refs):
    odd_x_in, refs = refs[6], refs[:6] + refs[7:]
    odd_x_out, refs = refs[9], refs[:9] + refs[10:]

    @pl.when(lax.axis_index("gx") == 0)
    def _():
        slope_body(rows, *refs)


def late_slope_kernel(rows, *refs):
    refs = refs[:6] + refs[9:]

    @pl.when(lax.axis_index("gx") != 0)
    def _():
        slope_body(rows, *refs)


def gather_kernel(
    rows, costate_ref, stream_ref, span_ref, coef_ref, even_z_ref, odd_z_ref, arrive_ref,
    partial_ref, values, arrived,
):
    count = 2 * fields
    half = rows // 2
    width = half * 8
    values[16:24] = jnp.zeros((8, values.shape[1]), jnp.float32)
    for c in range(fields):
        values[2 * c : 2 * c + 2] = even_z_ref[c]
        values[count + 2 * c : count + 2 * c + 2] = odd_z_ref[c]
    for part in range(2):
        whole = values[:, part * width : (part + 1) * width]
        top = whole.astype(jnp.bfloat16).astype(jnp.float32)
        stacked = jnp.concatenate([top, whole - top, top], 0)
        columns = jnp.swapaxes(stacked, 0, 1).astype(jnp.bfloat16)
        out = jnp.dot(columns, arrive_ref[...], preferred_element_type=jnp.float32)
        for c in range(fields):
            arrived[c, part * half : (part + 1) * half] = out[:, c * 128 : (c + 1) * 128].reshape(
                half, 8, 128
            )

    def add(i, carry):
        a = [stream_ref[c, i] for c in range(fields)]
        b = [span_ref[c, i] + arrived[c, i] for c in range(fields)]
        pulled = pull(a, b, *[coef_ref[slot, i] for slot in range(5)])
        for c in range(fields):
            partial_ref[c, i] = costate_ref[c, i] + pulled[c]
        return carry

    lax.fori_loop(0, rows, add, 0, unroll=16)


def pull_stream(a, u0, u1, u2, h, k):
    both = a[4] * u0
    g = (gas_gamma - 1.0) * (a[1] + both)
    a1u0 = a[1] * u0
    v0 = a1u0 + a[2] * u1 + a[3] * u2 + a[4] * h
    return [
        g * k - v0 * u0,
        a[0] + a1u0 + v0 - g * u0,
        a[2] * u0 - g * u1,
        a[3] * u0 - g * u2,
        both + g,
    ]


def join_kernel(rows, partial_ref, coef_ref, odd_x_ref, out_hbm, result, sems):
    place = lax.axis_index("gx") % 2
    per_segment = rows // pieces
    sign = jnp.where(place == 0, 1.0, -1.0).astype(jnp.float32)

    def copy_out(s):
        at = jnp.where(place == 0, s, pieces - 1 - s)
        part = pl.ds(at * per_segment, per_segment)
        return pltpu.make_async_copy(result.at[:, part], out_hbm.at[:, part], sems.at[s])

    def step(t, a):
        i = jnp.where(place == 0, t, rows - 1 - t)
        pulled = pull_stream(a, *[coef_ref[slot, i] for slot in range(5)])
        for c in range(fields):
            result[c, i] = partial_ref[c, i] + pulled[c]

    def segment(s, carry):
        for j in range(per_segment):
            now = carry
            if j == 0:
                edge = jnp.where(s == 0, -sign * (step_scale * side), 0.0).astype(jnp.float32)
                now = tuple(carry[c] + edge * odd_x_ref[c, 1] for c in range(fields))
            step(s * per_segment + j, now)
            carry = tuple(value * root for value in carry)
        copy_out(s).start()
        return carry

    total = tuple(odd_x_ref[c, 0] * (sign * (step_scale * tail)) for c in range(fields))
    lax.fori_loop(0, pieces, segment, total)

    def finish(s, carry):
        copy_out(s).wait()
        return carry

    lax.fori_loop(0, pieces, finish, 0)


def per_device(density, momentum, energy, costate):
    rows, planes, cells = density.shape
    f32 = jnp.float32
    whole = pl.BlockSpec(memory_space=pltpu.VMEM)
    hbm = pl.BlockSpec(memory_space=pltpu.HBM)
    params = pltpu.CompilerParams(vmem_limit_bytes=vmem_bytes)
    x_shape = jax.ShapeDtypeStruct((fields, 2, planes, cells), f32)
    z_shape = jax.ShapeDtypeStruct((fields, 2, rows * planes), f32)
    block = jax.ShapeDtypeStruct((fields, rows, planes, cells), f32)
    per_segment = rows // segments

    matrix = local_matrix(cells)
    arrive = stack_arrival(step_scale * arrival_rows(cells))
    held, even_x, even_z, odd_z, odd_x, matrix, arrive = pl.pallas_call(
        lambda *refs: ends_kernel(rows, *refs),
        out_shape=(
            jax.ShapeDtypeStruct((fields, segments, per_segment, planes, cells), f32),
            x_shape,
            z_shape,
            z_shape,
            x_shape,
            jax.ShapeDtypeStruct(matrix.shape, jnp.bfloat16),
            jax.ShapeDtypeStruct(arrive.shape[1:], jnp.bfloat16),
        ),
        in_specs=[hbm] * 4,
        out_specs=(whole,) * 7,
        scratch_shapes=[
            pltpu.VMEM((16, 2 * cells), jnp.bfloat16),
            pltpu.SemaphoreType.DMA((fields + 3,)),
        ],
        compiler_params=params,
        name="ends",
    )(
        in_hbm(costate.reshape(fields, segments, per_segment, planes, cells)),
        in_hbm(jnp.asarray(stack_ends(end_weights(cells)))),
        in_hbm(jnp.asarray(matrix)),
        in_hbm(jnp.asarray(arrive)),
    )
    held = held.reshape(costate.shape)

    def pairs(values, axis, odd):
        count = lax.axis_size(axis)
        links = []
        for i in range(odd, count + odd, 2):
            a, b = i % count, (i + 1) % count
            links += [(a, b), (b, a)]
        return lax.ppermute(values, axis, links)

    even_x = pairs(even_x, "gx", 0)
    even_z = pairs(even_z, "gz", 0)
    odd_z = pairs(odd_z, "gz", 1)

    state = (
        pltpu.VMEM((rows, planes, cells), f32),
        pltpu.VMEM((3, rows, planes, cells), f32),
        pltpu.VMEM((rows, planes, cells), f32),
    )
    inputs = (held, even_x, matrix, in_hbm(density), in_hbm(momentum), in_hbm(energy))
    stream, span, coef, odd_x = pl.pallas_call(
        lambda *refs: early_slope_kernel(rows, *refs),
        out_shape=(block, block, block, x_shape),
        in_specs=[whole] * 3 + [hbm] * 3 + [whole],
        out_specs=(whole,) * 4,
        scratch_shapes=[*state, pltpu.SemaphoreType.DMA((3,))],
        input_output_aliases={6: 3},
        compiler_params=params,
        name="early_slope",
    )(*inputs, odd_x)

    odd_x = pairs(odd_x, "gx", 1)

    stream, span, coef = pl.pallas_call(
        lambda *refs: late_slope_kernel(rows, *refs),
        out_shape=(block,) * 3,
        in_specs=[whole] * 3 + [hbm] * 3 + [whole] * 3,
        out_specs=(whole,) * 3,
        scratch_shapes=[*state, pltpu.SemaphoreType.DMA((3,))],
        input_output_aliases={6: 0, 7: 1, 8: 2},
        compiler_params=params,
        cost_estimate=pl.CostEstimate(flops=300_000_000, bytes_accessed=10_000_000, transcendentals=0),
        name="late_slope",
    )(*inputs, stream, span, coef)

    partial = pl.pallas_call(
        lambda *refs: gather_kernel(rows, *refs),
        out_shape=block,
        in_specs=[whole] * 7,
        out_specs=whole,
        scratch_shapes=[
            pltpu.VMEM((arrival_depth, rows * planes), f32),
            pltpu.VMEM((fields, rows, planes, cells), f32),
        ],
        compiler_params=params,
        cost_estimate=pl.CostEstimate(flops=100_000_000, bytes_accessed=10_000_000, transcendentals=0),
        name="gather",
    )(held, stream, span, coef, even_z, odd_z, arrive)

    return pl.pallas_call(
        lambda *refs: join_kernel(rows, *refs),
        out_shape=block,
        in_specs=[whole] * 3,
        out_specs=hbm,
        scratch_shapes=[
            pltpu.VMEM((fields, rows, planes, cells), f32),
            pltpu.SemaphoreType.DMA((pieces,)),
        ],
        compiler_params=params,
        name="join",
    )(partial, coef, odd_x)


def solution(mesh):
    return jax.shard_map(
        per_device,
        mesh=mesh,
        in_specs=(
            P("gx", None, "gz"),
            P(None, "gx", None, "gz"),
            P("gx", None, "gz"),
            P(None, "gx", None, "gz"),
        ),
        out_specs=P(None, "gx", None, "gz"),
        check_vma=False,
    )
```

```python
import math

import jax
import jax.numpy as jnp
import ml_dtypes
import numpy as np
from jax import lax
from jax.experimental import pallas as pl
from jax.experimental.pallas import tpu as pltpu
from jax.sharding import PartitionSpec as P

pade_alpha = 1.0 / 3.0
near_coef = 14.0 / 9.0
far_coef = 1.0 / 9.0
step_scale = 0.1
gas_gamma = 1.4

root = (-1.0 + math.sqrt(1.0 - 4.0 * pade_alpha * pade_alpha)) / (2.0 * pade_alpha)
side = 0.25 * far_coef / pade_alpha
tail = (0.5 * near_coef - side) / pade_alpha

fields = 5
segments = 8
pieces = 16
arrival_depth = 24
vmem_bytes = 16 * 1024 * 1024


def split(values):
    high = values.astype(ml_dtypes.bfloat16)
    low = (values - high.astype(np.float64)).astype(ml_dtypes.bfloat16)
    return high, low


def end_weights(length):
    cell = np.arange(length, dtype=np.float64)
    rows = np.zeros((4, length))
    rows[0] = root ** (length - cell)
    rows[1, length - 1] = 1.0
    rows[2] = root ** (cell + 1.0)
    rows[3, 0] = 1.0
    return rows


def stack_ends(rows):
    stacked = np.zeros((2, 16, 2 * rows.shape[1]), ml_dtypes.bfloat16)
    for place, order in enumerate(((0, 1, 2, 3), (2, 3, 0, 1))):
        high, low = split(rows[list(order)])
        stacked[place, 0:4] = np.concatenate([high, high], 1)
        stacked[place, 8:12] = np.concatenate([low, np.zeros_like(low)], 1)
    return stacked


def local_matrix(length):
    cell = np.arange(length)
    gap = cell[None, :] - cell[:, None]
    reach = np.abs(gap).astype(np.float64)
    taps = np.where(reach > 0, tail * root**reach, 0.0) - np.where(reach == 1, side, 0.0)
    high, low = split(step_scale * np.sign(gap) * taps)
    return np.concatenate(
        [np.concatenate([high, low], 1), np.concatenate([high, low], 1)], 0
    )


def arrival_rows(length):
    cell = np.arange(length, dtype=np.float64)
    rows = np.zeros((4, length))
    rows[0] = tail * root**cell
    rows[1, 0] = -side
    rows[2] = -tail * root ** (length - 1.0 - cell)
    rows[3, length - 1] = side
    return rows


def stack_arrival(rows):
    length = rows.shape[1]
    stacked = np.zeros((2, 3 * arrival_depth, fields * length), ml_dtypes.bfloat16)
    for place, order in enumerate(((2, 3, 0, 1), (0, 1, 2, 3))):
        high, low = split(rows[list(order)])
        for n in range(4):
            for c in range(fields):
                at = (n // 2) * 2 * fields + 2 * c + n % 2
                lanes = slice(c * length, (c + 1) * length)
                stacked[place, at, lanes] = high[n]
                stacked[place, arrival_depth + at, lanes] = high[n]
                stacked[place, 2 * arrival_depth + at, lanes] = low[n]
    return stacked


def in_hbm(values):
    return pltpu.with_memory_space_constraint(values, pltpu.HBM)


def ends_kernel(
    rows, costate_hbm, weights_hbm, matrix_hbm, arrive_hbm, held, even_x_ref, even_z_ref, odd_z_ref,
    odd_x_ref, matrix_ref, arrive_ref, weights_ref, sems,
):
    per_segment = rows // segments
    place = lax.axis_index("gz") % 2
    constants = [
        pltpu.make_async_copy(source, target, sems.at[fields + n])
        for n, (source, target) in enumerate(
            (
                (weights_hbm.at[place], weights_ref),
                (matrix_hbm, matrix_ref),
                (arrive_hbm.at[place], arrive_ref),
            )
        )
    ]
    constants[0].start()
    for c in range(fields):
        pltpu.make_async_copy(costate_hbm.at[c], held.at[c], sems.at[c]).start()
    constants[1].start()
    constants[2].start()
    x_even = lax.axis_index("gx") % 2 == 0
    constants[0].wait()

    def component(c, carry):
        pltpu.make_async_copy(costate_hbm.at[c], held.at[c], sems.at[c]).wait()
        lines = held[c].reshape(-1, 128)
        high = lines.astype(jnp.bfloat16)
        low = (lines - high.astype(jnp.float32)).astype(jnp.bfloat16)
        sums = lax.dot_general(
            weights_ref[...],
            jnp.concatenate([high, low], 1),
            (((1,), (1,)), ((), ())),
            preferred_element_type=jnp.float32,
        )
        sums = sums[0:8] + sums[8:16]
        even_z_ref[c] = sums[0:2]
        odd_z_ref[c] = sums[2:4]
        ahead = held[c, :, 0]
        back = held[c, :, per_segment - 1]
        for j in range(1, per_segment):
            ahead = ahead * root + held[c, :, j]
            back = back * root + held[c, :, per_segment - 1 - j]
        right = [ahead[segments - 1 - s] * float(root ** (1 + s * per_segment)) for s in range(segments)]
        left = [back[s] * float(root ** (1 + s * per_segment)) for s in range(segments)]
        while len(right) > 1:
            right = [right[n] + right[n + 1] for n in range(0, len(right), 2)]
            left = [left[n] + left[n + 1] for n in range(0, len(left), 2)]
        first = held[c, 0, 0]
        last = held[c, segments - 1, per_segment - 1]
        even_x_ref[c, 0] = jnp.where(x_even, right[0], left[0])
        even_x_ref[c, 1] = jnp.where(x_even, last, first)
        odd_x_ref[c, 0] = jnp.where(x_even, left[0], right[0])
        odd_x_ref[c, 1] = jnp.where(x_even, first, last)
        return carry

    lax.fori_loop(0, fields, component, 0)
    constants[1].wait()
    constants[2].wait()


def pull(a, b, u0, u1, u2, h, k):
    a4u0 = a[4] * u0
    b4u2 = b[4] * u2
    both = a4u0 + b4u2
    g = (gas_gamma - 1.0) * (a[1] + b[3] + both)
    a1u0 = a[1] * u0
    b3u2 = b[3] * u2
    v0 = a1u0 + a[2] * u1 + a[3] * u2 + a[4] * h
    v2 = b[1] * u0 + b[2] * u1 + b3u2 + b[4] * h
    mass = g * k - v0 * u0 - v2 * u2
    m0 = a[0] + a1u0 + b[1] * u2 + v0 - g * u0
    m1 = a[2] * u0 + b[2] * u2 - g * u1
    m2 = b[0] + a[3] * u0 + b3u2 + v2 - g * u2
    energy = both + g
    return [mass, m0, m1, m2, energy]


def slope_body(
    rows, costate_ref, even_x_ref, matrix_ref, density_hbm, momentum_hbm, energy_hbm,
    stream_ref, span_ref, coef_ref, density_ref, momentum_ref, energy_ref, sems,
):
    half = rows // 2
    copies = []
    for part in range(2):
        at = pl.ds(part * half, half)
        for n, (source, target) in enumerate(
            (
                (density_hbm.at[at], density_ref.at[at]),
                (momentum_hbm.at[:, at], momentum_ref.at[:, at]),
                (energy_hbm.at[at], energy_ref.at[at]),
            )
        ):
            copies.append(pltpu.make_async_copy(source, target, sems.at[3 * part + n]))
    for copy in copies:
        copy.start()
    x_even = lax.axis_index("gx") % 2 == 0
    gain = step_scale * tail
    edge = step_scale * side
    from_right = jnp.where(x_even, 1.0, 0.0).astype(jnp.float32)
    from_left = 1.0 - from_right
    right_sum = tuple(even_x_ref[c, 0] * (from_right * gain) for c in range(fields))
    for c in range(fields):
        stream_ref[c, rows - 1] = right_sum[c] - even_x_ref[c, 1] * (from_right * edge)

    def backward(step, carry):
        i = rows - 2 - step
        nxt = []
        for c in range(fields):
            after = costate_ref[c, i + 1]
            now = carry[c] * root + after * (gain * root)
            stream_ref[c, i] = now - after * edge
            nxt.append(now)
        return tuple(nxt)

    lax.fori_loop(0, rows - 1, backward, right_sum, unroll=8)

    def across(c, carry):
        lines = costate_ref[...].reshape(-1, 128)
        high = lines.astype(jnp.bfloat16)
        low = (lines - high.astype(jnp.float32)).astype(jnp.bfloat16)
        out = jnp.dot(
            jnp.concatenate([high, low], 1), matrix_ref[...], preferred_element_type=jnp.float32
        )
        span_ref[...] = (out[:, :128] + out[:, 128:]).reshape(fields, rows, 8, 128)
        return carry

    across(0, 0)
    def forward(i, carry):
        ahead, before = carry
        ahead = tuple(ahead[c] * root + before[c] * (gain * root) for c in range(fields))
        for c in range(fields):
            stream_ref[c, i] = ahead[c] - before[c] * edge - stream_ref[c, i]
        return ahead, tuple(costate_ref[c, i] for c in range(fields))

    before = tuple(even_x_ref[c, 1] * from_left for c in range(fields))
    ahead = tuple(
        (even_x_ref[c, 0] * (from_left / root) - before[c]) * gain for c in range(fields)
    )
    lax.fori_loop(0, rows, forward, (ahead, before), unroll=8)

    def state(i, carry):
        rho = density_ref[i]
        inverse = pl.reciprocal(rho, approx=True)
        inverse = inverse * (2.0 - rho * inverse)
        u0 = momentum_ref[0, i] * inverse
        u1 = momentum_ref[1, i] * inverse
        u2 = momentum_ref[2, i] * inverse
        k = 0.5 * (u0 * u0 + u1 * u1 + u2 * u2)
        h = gas_gamma * (energy_ref[i] * inverse) - (gas_gamma - 1.0) * k
        for slot, value in enumerate((u0, u1, u2, h, k)):
            coef_ref[slot, i] = value
        return carry

    for part in range(2):
        for copy in copies[3 * part : 3 * part + 3]:
            copy.wait()
        lax.fori_loop(part * half, (part + 1) * half, state, 0, unroll=8)


def early_slope_kernel(rows, *refs):
    odd_x_in, refs = refs[6], refs[:6] + refs[7:]
    odd_x_out, refs = refs[9], refs[:9] + refs[10:]

    @pl.when(lax.axis_index("gx") == 0)
    def _():
        slope_body(rows, *refs)


def late_slope_kernel(rows, *refs):
    refs = refs[:6] + refs[9:]

    @pl.when(lax.axis_index("gx") != 0)
    def _():
        slope_body(rows, *refs)


def gather_kernel(
    rows, costate_ref, stream_ref, span_ref, coef_ref, even_z_ref, odd_z_ref, arrive_ref,
    partial_ref, values, arrived,
):
    count = 2 * fields
    half = rows // 2
    width = half * 8
    values[16:24] = jnp.zeros((8, values.shape[1]), jnp.float32)
    for c in range(fields):
        values[2 * c : 2 * c + 2] = even_z_ref[c]
        values[count + 2 * c : count + 2 * c + 2] = odd_z_ref[c]
    for part in range(2):
        whole = values[:, part * width : (part + 1) * width]
        top = whole.astype(jnp.bfloat16).astype(jnp.float32)
        stacked = jnp.concatenate([top, whole - top, top], 0)
        columns = jnp.swapaxes(stacked, 0, 1).astype(jnp.bfloat16)
        out = jnp.dot(columns, arrive_ref[...], preferred_element_type=jnp.float32)
        for c in range(fields):
            arrived[c, part * half : (part + 1) * half] = out[:, c * 128 : (c + 1) * 128].reshape(
                half, 8, 128
            )

    def add(i, carry):
        a = [stream_ref[c, i] for c in range(fields)]
        b = [span_ref[c, i] + arrived[c, i] for c in range(fields)]
        pulled = pull(a, b, *[coef_ref[slot, i] for slot in range(5)])
        for c in range(fields):
            partial_ref[c, i] = costate_ref[c, i] + pulled[c]
        return carry

    lax.fori_loop(0, rows, add, 0, unroll=16)


def pull_stream(a, u0, u1, u2, h, k):
    both = a[4] * u0
    g = (gas_gamma - 1.0) * (a[1] + both)
    a1u0 = a[1] * u0
    v0 = a1u0 + a[2] * u1 + a[3] * u2 + a[4] * h
    return [
        g * k - v0 * u0,
        a[0] + a1u0 + v0 - g * u0,
        a[2] * u0 - g * u1,
        a[3] * u0 - g * u2,
        both + g,
    ]


def join_kernel(rows, partial_ref, coef_ref, odd_x_ref, out_hbm, result, sems):
    place = lax.axis_index("gx") % 2
    per_segment = rows // pieces
    sign = jnp.where(place == 0, 1.0, -1.0).astype(jnp.float32)

    def copy_out(s):
        at = jnp.where(place == 0, s, pieces - 1 - s)
        part = pl.ds(at * per_segment, per_segment)
        return pltpu.make_async_copy(result.at[:, part], out_hbm.at[:, part], sems.at[s])

    def step(t, a):
        i = jnp.where(place == 0, t, rows - 1 - t)
        pulled = pull_stream(a, *[coef_ref[slot, i] for slot in range(5)])
        for c in range(fields):
            result[c, i] = partial_ref[c, i] + pulled[c]

    def segment(s, carry):
        for j in range(per_segment):
            now = carry
            if j == 0:
                edge = jnp.where(s == 0, -sign * (step_scale * side), 0.0).astype(jnp.float32)
                now = tuple(carry[c] + edge * odd_x_ref[c, 1] for c in range(fields))
            step(s * per_segment + j, now)
            carry = tuple(value * root for value in carry)
        copy_out(s).start()
        return carry

    total = tuple(odd_x_ref[c, 0] * (sign * (step_scale * tail)) for c in range(fields))
    lax.fori_loop(0, pieces, segment, total)

    def finish(s, carry):
        copy_out(s).wait()
        return carry

    lax.fori_loop(0, pieces, finish, 0)


def per_device(density, momentum, energy, costate):
    rows, planes, cells = density.shape
    f32 = jnp.float32
    whole = pl.BlockSpec(memory_space=pltpu.VMEM)
    hbm = pl.BlockSpec(memory_space=pltpu.HBM)
    params = pltpu.CompilerParams(vmem_limit_bytes=vmem_bytes)
    x_shape = jax.ShapeDtypeStruct((fields, 2, planes, cells), f32)
    z_shape = jax.ShapeDtypeStruct((fields, 2, rows * planes), f32)
    block = jax.ShapeDtypeStruct((fields, rows, planes, cells), f32)
    per_segment = rows // segments

    matrix = local_matrix(cells)
    arrive = stack_arrival(step_scale * arrival_rows(cells))
    held, even_x, even_z, odd_z, odd_x, matrix, arrive = pl.pallas_call(
        lambda *refs: ends_kernel(rows, *refs),
        out_shape=(
            jax.ShapeDtypeStruct((fields, segments, per_segment, planes, cells), f32),
            x_shape,
            z_shape,
            z_shape,
            x_shape,
            jax.ShapeDtypeStruct(matrix.shape, jnp.bfloat16),
            jax.ShapeDtypeStruct(arrive.shape[1:], jnp.bfloat16),
        ),
        in_specs=[hbm] * 4,
        out_specs=(whole,) * 7,
        scratch_shapes=[
            pltpu.VMEM((16, 2 * cells), jnp.bfloat16),
            pltpu.SemaphoreType.DMA((fields + 3,)),
        ],
        compiler_params=params,
        name="ends",
    )(
        in_hbm(costate.reshape(fields, segments, per_segment, planes, cells)),
        in_hbm(jnp.asarray(stack_ends(end_weights(cells)))),
        in_hbm(jnp.asarray(matrix)),
        in_hbm(jnp.asarray(arrive)),
    )
    held = held.reshape(costate.shape)

    def pairs(values, axis, odd):
        count = lax.axis_size(axis)
        links = []
        for i in range(odd, count + odd, 2):
            a, b = i % count, (i + 1) % count
            links += [(a, b), (b, a)]
        return lax.ppermute(values, axis, links)

    even_x = pairs(even_x, "gx", 0)
    even_z = pairs(even_z, "gz", 0)
    odd_z = pairs(odd_z, "gz", 1)

    state = (
        pltpu.VMEM((rows, planes, cells), f32),
        pltpu.VMEM((3, rows, planes, cells), f32),
        pltpu.VMEM((rows, planes, cells), f32),
    )
    inputs = (held, even_x, matrix, in_hbm(density), in_hbm(momentum), in_hbm(energy))
    stream, span, coef, odd_x = pl.pallas_call(
        lambda *refs: early_slope_kernel(rows, *refs),
        out_shape=(block, block, block, x_shape),
        in_specs=[whole] * 3 + [hbm] * 3 + [whole],
        out_specs=(whole,) * 4,
        scratch_shapes=[*state, pltpu.SemaphoreType.DMA((6,))],
        input_output_aliases={6: 3},
        compiler_params=params,
        name="early_slope",
    )(*inputs, odd_x)

    odd_x = pairs(odd_x, "gx", 1)

    stream, span, coef = pl.pallas_call(
        lambda *refs: late_slope_kernel(rows, *refs),
        out_shape=(block,) * 3,
        in_specs=[whole] * 3 + [hbm] * 3 + [whole] * 3,
        out_specs=(whole,) * 3,
        scratch_shapes=[*state, pltpu.SemaphoreType.DMA((6,))],
        input_output_aliases={6: 0, 7: 1, 8: 2},
        compiler_params=params,
        cost_estimate=pl.CostEstimate(flops=300_000_000, bytes_accessed=10_000_000, transcendentals=0),
        name="late_slope",
    )(*inputs, stream, span, coef)

    partial = pl.pallas_call(
        lambda *refs: gather_kernel(rows, *refs),
        out_shape=block,
        in_specs=[whole] * 7,
        out_specs=whole,
        scratch_shapes=[
            pltpu.VMEM((arrival_depth, rows * planes), f32),
            pltpu.VMEM((fields, rows, planes, cells), f32),
        ],
        compiler_params=params,
        cost_estimate=pl.CostEstimate(flops=100_000_000, bytes_accessed=10_000_000, transcendentals=0),
        name="gather",
    )(held, stream, span, coef, even_z, odd_z, arrive)

    return pl.pallas_call(
        lambda *refs: join_kernel(rows, *refs),
        out_shape=block,
        in_specs=[whole] * 3,
        out_specs=hbm,
        scratch_shapes=[
            pltpu.VMEM((fields, rows, planes, cells), f32),
            pltpu.SemaphoreType.DMA((pieces,)),
        ],
        compiler_params=params,
        name="join",
    )(partial, coef, odd_x)


def solution(mesh):
    return jax.shard_map(
        per_device,
        mesh=mesh,
        in_specs=(
            P("gx", None, "gz"),
            P(None, "gx", None, "gz"),
            P("gx", None, "gz"),
            P(None, "gx", None, "gz"),
        ),
        out_specs=P(None, "gx", None, "gz"),
        check_vma=False,
    )
```
